32 devices in a mesh: parts: 2 (over y), region: 8 (over z, x), narrow: 2 (over core).
Axes of the slice: x: 2, y: 2, z: 4, core: 2. Of those that a mesh axis runs over, the one named last changes fastest.
Arguments:
- queries: bfloat16 [4096, 1024], P(('parts', 'region', 'narrow')), parts along dimension 0, may hold values from -6 to 6
- probes: int32 [4096, 4], P(('parts', 'region', 'narrow')), parts along dimension 0, may hold values from 0 to 7, all different within a row; in each aligned block of 128 rows (0 to 127, 128 to 255, ...) at most 128 rows name the same one
- fine_blocks: int32 [4096, 4, 4], P(('parts', 'region', 'narrow')), parts along dimension 0, may hold values from 0 to 15, as said below
- centroids: bfloat16 [8, 2048, 1024], P('region', 'narrow'), may hold values from -6 to 6
Outputs:
- scores: bfloat16 [4096, 4, 512], P(('parts', 'region', 'narrow')), parts along dimension 0
The draws below stay inside these ranges and needn't reach their ends.
There are 2 independent parts, one for each index of `parts`. The reference program is written for one: setup_inputs(seed, part) draws one part's arguments, and reference() takes and returns one part's arrays. A program takes and returns all parts, laid end to end along the dimension named above; an argument that names none is the same for every part. Nothing has to cross between parts.
Inputs may be any that keep to these rules, and one draw needn't show every extreme that they name: `probes`: a query's 4 regions differ; of the 128 x 4 entries of one device's queries at most 128 name one region. `fine_blocks`: the 4 blocks of one query and probe differ.
All inputs are finite; a program needn't handle non-finite values.
Results may differ from the reference program's by a relative error of at most 0.001.
Values may be sent and summed in bfloat16 or wider, within the bound.
No kernel may reach another device: no remote copies, remote signals or barrier semaphores. Data moves between devices by JAX's collectives and lax.ppermute only.
A program may use at most 64 MiB of HBM per device.

```python
import math
from functools import partial
import jax
import jax.numpy as jnp
import numpy as np
from jax import lax

D = 1024
BLK = 128
BLOCKS = 16
NACT = 4
PROBE = 4
Q_DEV = 128
REGIONS = 8
CENT = 2048
QUERIES = 2048
CAP = 128


def draw_fine_blocks(key, part):
    key = jax.random.fold_in(key, 7)
    ranked = jax.random.randint(key, (QUERIES, PROBE, BLOCKS), 0, 2 ** 20) * BLOCKS
    ranked = ranked + jnp.arange(BLOCKS, dtype=jnp.int32)
    order_ids = jnp.argsort(ranked, axis=-1)
    return order_ids[..., :NACT].astype(jnp.int32)


def level_of(own_key, extent, split, smallest, top_value):
    level = 1.0
    for dim, blocks in split:
        heights = jax.random.uniform(jax.random.fold_in(jax.random.fold_in(own_key, 6), dim), (blocks,), jnp.float32, smallest / len(split), top_value / len(split))
        level = level * jnp.repeat(jnp.exp(heights), extent[dim] // blocks).reshape((-1,) + (1,) * (len(extent) - 1 - dim))
    return level


def assign_block(own_key, own, number, rows, number_of, top, most, lean):
    order = jax.random.permutation(own_key, number_of)
    crowded, ordinary = load_shares(number_of, rows * top, most, lean, True), load_shares(number_of, rows * top, most, lean, False)
    places = jnp.arange(number_of)

    def named(tallies, offset_by):
        used = int((tallies > 0).sum())
        fixed = max(1, used // 4)
        moved = fixed + (places - fixed + offset_by * (used - fixed)) % max(1, number_of - fixed)
        return jnp.zeros((number_of,), jnp.int32).at[order[jnp.where(places < fixed, places, moved)]].set(jnp.asarray(tallies, jnp.int32))

    tallies = jnp.where(number % 4 == 0, named(crowded, number // 4), named(ordinary, number - number // 4 - 1))
    mixed = jax.random.permutation(jax.random.fold_in(own, 3), number_of)
    donor, sink = mixed[0:number_of // 2 * 2:2], mixed[1:number_of // 2 * 2:2]
    margin = jnp.minimum(tallies[donor] - 1, most - tallies[sink]) // 2
    margin = jnp.where((donor == order[0]) | (sink == order[0]) | (tallies[sink] == 0), 0, jnp.maximum(margin, 0))
    moved = jax.random.randint(jax.random.fold_in(own, 4), (number_of // 2,), 0, 1 << 20) % (margin + 1)
    tallies = tallies.at[donor].add(-moved).at[sink].add(moved)
    labels = jnp.searchsorted(jnp.cumsum(tallies), jnp.arange(rows * top), side="right").astype(jnp.int32)
    listing = labels.reshape(top, rows).T
    listing = listing[jax.random.permutation(jax.random.fold_in(own, 1), rows)]
    offset_by = jax.random.randint(jax.random.fold_in(own, 2), (rows, 1), 0, top)
    return jnp.take_along_axis(listing, (jnp.arange(top)[None, :] + offset_by) % top, axis=1)


def load_shares(count, total, most, slope, full):
    weights = [(1 << 20) // math.isqrt(rank ** slope) + 1 for rank in range(1, count + 1)]
    largest = most if full else min(most, max(-(-total // count), total * weights[0] // sum(weights)))
    least = 1 if total - largest >= count - 1 else 0
    holding, surplus = [largest] + [least] * (count - 1), total - largest - least * (count - 1)
    while surplus > 0:
        movable = [i for i in range(1, count) if holding[i] < largest] or [i for i in range(1, count) if holding[i] < most]
        whole, remaining = sum([weights[i] for i in movable]), surplus
        for i in movable:
            more = min(most - holding[i], max(1, remaining * weights[i] // whole), surplus)
            holding[i] = holding[i] + more
            surplus = surplus - more
    return np.array(holding)


def bell_draw(stream_key, dims, deviation, bound, cuts=(), held_as=jnp.bfloat16):
    array = jax.random.normal(stream_key, dims, jnp.float32) * deviation
    if len(cuts) > 0:
        array = level_of(stream_key, dims, cuts, -0.22, 0.18) * array
    return jnp.clip(array, min=-bound, max=bound).astype(held_as)


def setup_inputs(seed: int = 0, part: int = 0) -> dict:
    key_of = jax.random.split(jax.random.key(seed), 5)
    part_keys = jax.random.split(jax.random.fold_in(key_of[4], part), 5)
    queries = bell_draw(part_keys[0], (QUERIES, D), 1.0, 6.0, ((0, 16),))
    probes_keys = jax.random.split(jax.random.fold_in(part_keys[1], 1), QUERIES // Q_DEV)
    probes_turns = jax.random.permutation(jax.random.fold_in(part_keys[1], 3), QUERIES // Q_DEV)
    probes = jax.vmap(lambda own, number: assign_block(jax.random.fold_in(part_keys[1], 2), own, number, Q_DEV, REGIONS, PROBE, CAP, 2))(probes_keys, probes_turns).reshape((QUERIES, PROBE))
    fine_blocks = draw_fine_blocks(jax.random.fold_in(jax.random.fold_in(key_of[4], part), 71), part)
    centroids = bell_draw(key_of[3], (REGIONS, CENT, D), 1.0, 6.0, ((0, 8), (1, 2)))
    return {"queries": queries, "probes": probes, "fine_blocks": fine_blocks, "centroids": centroids}


def score_batch(batched, cblocks):
    q_batch, p_batch, f_batch = batched
    chosen = cblocks[p_batch[:, :, None], f_batch].astype(jnp.float32)
    inner_prod = jnp.einsum('bd,bpnkd->bpnk', q_batch.astype(jnp.float32), chosen)
    sq_norm = lax.optimization_barrier(jnp.sum(chosen * chosen, axis=-1))
    scored = inner_prod / math.sqrt(D) - 0.5 * sq_norm / D
    return scored.reshape(q_batch.shape[0], PROBE, NACT * BLK).astype(jnp.bfloat16)

def reference(queries, probes, fine_blocks, centroids):
    cblocks = centroids.reshape(REGIONS, BLOCKS, BLK, D)
    per_step = 8
    steps_count = QUERIES // per_step
    shaped = (queries.reshape(steps_count, per_step, D), probes.reshape(steps_count, per_step, PROBE), fine_blocks.reshape(steps_count, per_step, PROBE, NACT))
    result = lax.map(partial(score_batch, cblocks=cblocks), shaped)
    return result.reshape(QUERIES, PROBE, NACT * BLK)
```

```python
import functools
import math

import jax
import jax.numpy as jnp
from jax import lax
from jax.experimental import pallas as pl
from jax.experimental.pallas import tpu as pltpu
from jax.sharding import PartitionSpec as P

BLK = 128


def score_against(flat_rows, centre_rows):
    inner_prod = jnp.einsum("nd,md->nm", flat_rows, centre_rows, preferred_element_type=jnp.float32)
    widened = centre_rows.astype(jnp.float32)
    sq_norm = jnp.sum(widened * widened, axis=1)
    width = flat_rows.shape[1]
    return inner_prod / math.sqrt(width) - 0.5 * sq_norm[None, :] / width


def pick_blocks(scored, block_ids, block_len):
    row_count = scored.shape[0]
    blocked = scored.reshape(row_count, -1, block_len)
    block_total = blocked.shape[1]
    chooser = (
        block_ids[:, :, None] == jnp.arange(block_total, dtype=jnp.int32)[None, None, :]
    ).astype(jnp.float32)
    selected = jnp.einsum("rjb,rbk->rjk", chooser, blocked, precision=lax.Precision.HIGHEST)
    return selected.reshape(row_count, -1)


def by_slots(queries, probes, fine_blocks, centroids):
    q_count, probe_count = probes.shape
    n_active = fine_blocks.shape[2]
    width = queries.shape[1]
    regions = lax.axis_size("region")
    capacity = max(2, min(q_count, 2 * q_count * probe_count // regions))
    slot_count = q_count * probe_count
    target_region = probes.reshape(slot_count)
    one_hot = (target_region[:, None] == jnp.arange(regions, dtype=jnp.int32)[None, :]).astype(
        jnp.float32
    )
    slot_index = jnp.arange(slot_count, dtype=jnp.int32)
    strict_lower = (slot_index[:, None] > slot_index[None, :]).astype(jnp.float32)
    earlier = jnp.dot(
        strict_lower, one_hot, precision=lax.Precision.HIGHEST, preferred_element_type=jnp.float32
    )
    slot_pos = jnp.sum(earlier * one_hot, axis=1).astype(jnp.int32)
    target_slot = target_region * capacity + slot_pos
    slot_match = jnp.arange(regions * capacity, dtype=jnp.int32)[:, None] == target_slot[None, :]
    query_match = jnp.any(
        slot_match.reshape(regions * capacity, q_count, probe_count), axis=2
    ).astype(jnp.bfloat16)
    send_rows = jnp.dot(query_match, queries, preferred_element_type=jnp.float32).astype(
        jnp.bfloat16
    )
    send_rows = send_rows.reshape(regions, capacity, width)
    block_values = fine_blocks.reshape(slot_count, n_active).astype(jnp.float32)
    send_blocks = jnp.dot(
        slot_match.astype(jnp.float32),
        block_values,
        precision=lax.Precision.HIGHEST,
        preferred_element_type=jnp.float32,
    ).astype(jnp.int32)
    send_blocks = send_blocks.reshape(regions, capacity, n_active)
    local_centres = centroids[0]
    in_rows = lax.all_to_all(send_rows, "region", split_axis=0, concat_axis=0, tiled=True)
    in_blocks = lax.all_to_all(send_blocks, "region", split_axis=0, concat_axis=0, tiled=True)
    sender_count = in_rows.shape[0]
    item_count = in_rows.shape[1]
    flat_rows = in_rows.reshape(sender_count * item_count, width)
    flat_blocks = in_blocks.reshape(sender_count * item_count, n_active)
    scored = score_against(flat_rows, lax.all_gather(local_centres, "narrow", axis=0, tiled=True))
    packed = pick_blocks(scored, flat_blocks, BLK).astype(jnp.bfloat16)
    packed = packed.reshape(sender_count, item_count, n_active * BLK)
    returned_all = lax.all_to_all(packed, "region", split_axis=0, concat_axis=0, tiled=True)
    flat_returned = returned_all.reshape(regions * capacity, -1)
    answers = jnp.dot(
        slot_match.T.astype(jnp.bfloat16), flat_returned, preferred_element_type=jnp.float32
    ).astype(jnp.bfloat16)
    return answers.reshape(q_count, probe_count, -1)


def choose(options, index):
    bit = 1
    while len(options) > 1:
        odd = (index & bit) != 0
        options = [
            jnp.where(odd, options[i + 1], options[i]) for i in range(0, len(options), 2)
        ]
        bit *= 2
    return options[0]


def score_kernel(
    n_sets, q_count, probe_count, n_active, scale, where_ref, *refs
):
    q_refs, meta_refs = refs[:n_sets], refs[n_sets : 2 * n_sets]
    own_ref, other_ref, own_bias_ref, other_bias_ref = refs[2 * n_sets : 2 * n_sets + 4]
    out_refs = refs[2 * n_sets + 4 : 3 * n_sets + 4]
    held = refs[3 * n_sets + 4]
    step = pl.program_id(0)
    rows = jnp.concatenate([r[...] for r in q_refs], axis=0)
    for side, (c_ref, b_ref) in enumerate(((own_ref, own_bias_ref), (other_ref, other_bias_ref))):
        inner = lax.dot_general(
            rows, c_ref[...], (((1,), (1,)), ((), ())), preferred_element_type=jnp.float32
        )
        held[side, step] = inner + b_ref[...]

    @pl.when(step == pl.num_programs(0) - 1)
    def _():
        region = where_ref[0].astype(jnp.float32)
        side_bit = where_ref[1] * (2 * held.shape[1] * held.shape[3] // BLK // 2)
        blocks = [
            (side, t, h)
            for side in range(2)
            for t in range(held.shape[1])
            for h in range(held.shape[3] // BLK)
        ]
        for s in range(n_sets):
            meta = meta_refs[s][...].astype(jnp.float32)
            wanted = jnp.zeros((n_active, q_count), jnp.float32)
            for p in range(probe_count):
                fine = meta[probe_count + p * n_active : probe_count + (p + 1) * n_active]
                wanted = wanted + jnp.where(meta[p : p + 1] == region, fine, 0.0)
            wanted = jnp.concatenate(
                [wanted, jnp.zeros((q_count - n_active, q_count), jnp.float32)], axis=0
            )
            columns = jnp.transpose(wanted).astype(jnp.int32) ^ side_bit
            step_rows = 32
            for r in range(0, q_count, step_rows):
                options = [
                    held[
                        side,
                        t,
                        s * q_count + r : s * q_count + r + step_rows,
                        h * BLK : (h + 1) * BLK,
                    ]
                    for side, t, h in blocks
                ]
                for j in range(n_active):
                    best = choose(options, columns[r : r + step_rows, j : j + 1])
                    out_refs[s][r : r + step_rows, j * BLK : (j + 1) * BLK] = (
                        best * scale
                    ).astype(jnp.bfloat16)


def score(where, blocks, metas, own, other, own_bias, other_bias, probe_count, n_active):
    n_sets = len(blocks)
    q_count, width = blocks[0].shape
    half = own.shape[0]
    tile = 256
    tiles = half // tile
    whole = lambda a: pl.BlockSpec(a.shape, lambda t, w: (0,) * a.ndim)
    out = jax.ShapeDtypeStruct((q_count, n_active * BLK), jnp.bfloat16)
    return pl.pallas_call(
        functools.partial(
            score_kernel, n_sets, q_count, probe_count, n_active, 1.0 / math.sqrt(width)
        ),
        out_shape=[out] * n_sets,
        grid_spec=pltpu.PrefetchScalarGridSpec(
            num_scalar_prefetch=1,
            grid=(tiles,),
            in_specs=[whole(b) for b in blocks]
            + [whole(m) for m in metas]
            + [pl.BlockSpec((tile, width), lambda t, w: (t, 0))] * 2
            + [pl.BlockSpec((1, tile), lambda t, w: (0, t))] * 2,
            out_specs=[whole(out)] * n_sets,
            scratch_shapes=[pltpu.VMEM((2, tiles, n_sets * q_count, tile), jnp.float32)],
        ),
        compiler_params=pltpu.CompilerParams(vmem_limit_bytes=24 * 1024 * 1024),
        cost_estimate=pl.CostEstimate(
            flops=2 * n_sets * q_count * 2 * half * width,
            bytes_accessed=2 * half * width * 2 + n_sets * q_count * (width + n_active * BLK) * 2,
            transcendentals=0,
        ),
        name="score",
    )(where, *blocks, *metas, own, other, own_bias, other_bias)


def answer_kernel(probe_count, regions, where_ref, probes_ref, *refs):
    part_refs, out_ref = refs[:regions], refs[regions]
    q_count = probes_ref.shape[0]
    step_rows = 16
    for r in range(0, q_count, step_rows):
        offset = probes_ref[r : r + step_rows, :] ^ where_ref[0]
        options = [p[r : r + step_rows, :].astype(jnp.float32) for p in part_refs]
        for p in range(probe_count):
            best = choose(options, offset[:, p : p + 1])
            out_ref[r : r + step_rows, p, :] = best.astype(jnp.bfloat16)


def answer(where, probes, parts):
    q_count, probe_count = probes.shape
    length = parts[0].shape[1]
    return pl.pallas_call(
        functools.partial(answer_kernel, probe_count, len(parts)),
        out_shape=jax.ShapeDtypeStruct((q_count, probe_count, length), jnp.bfloat16),
        in_specs=[pl.BlockSpec(memory_space=pltpu.SMEM)]
        + [pl.BlockSpec(memory_space=pltpu.VMEM)] * (1 + len(parts)),
        out_specs=pl.BlockSpec(memory_space=pltpu.VMEM),
        compiler_params=pltpu.CompilerParams(vmem_limit_bytes=24 * 1024 * 1024),
        name="answer",
    )(where, probes, *parts)


def by_blocks(queries, probes, fine_blocks, centroids):
    q_count, probe_count = probes.shape
    n_active = fine_blocks.shape[2]
    width = queries.shape[1]
    regions = lax.axis_size("region")

    def hop(value, mask):
        return lax.ppermute(value, "region", [(r, r ^ mask) for r in range(regions)])

    region = lax.axis_index("region")
    side = lax.axis_index("narrow")
    where = jnp.stack([region, side]).astype(jnp.int32)
    own = centroids[0]
    held = {0: queries}
    held[4] = hop(queries, 4)
    held[2] = hop(queries, 2)
    held[1] = hop(queries, 1)
    ids = jnp.concatenate([probes, fine_blocks.reshape(q_count, -1)], axis=1)
    ids = jnp.pad(ids.T.astype(jnp.bfloat16), ((0, -ids.shape[1] % 16), (0, 0)))
    ids_4 = hop(ids, 4)
    half_ids = jnp.stack([ids, ids_4])
    ids_2 = hop(half_ids, 2)
    most_ids = jnp.concatenate([half_ids, ids_2])
    ids_1 = hop(most_ids, 1)
    all_ids = dict(zip((0, 4, 2, 6, 1, 5, 3, 7), [*most_ids, *ids_1]))
    other = lax.ppermute(own, "narrow", [(0, 1), (1, 0)])
    factor = -0.5 / math.sqrt(width)
    bias = lambda c: (factor * jnp.sum(jnp.square(c.astype(jnp.float32)), axis=1))[None, :]
    own_bias, other_bias = bias(own), bias(other)
    scored = lambda *keys: dict(
        zip(
            keys,
            score(
                where,
                [held[k] for k in keys],
                [all_ids[k] for k in keys],
                own,
                other,
                own_bias,
                other_bias,
                probe_count,
                n_active,
            ),
        )
    )
    held[6] = hop(held[4], 2)
    held[5] = hop(held[4], 1)
    held[3] = hop(held[1], 2)
    held[7] = hop(held[6], 1)
    results = {}
    for keys in ((0, 4), (5, 6), (1, 2), (3, 7)):
        results.update(scored(*keys))
    parts = [results[0]] + [hop(results[k], k) for k in range(1, regions)]
    return answer(where, probes, parts)


def per_device(queries, probes, fine_blocks, centroids):
    q_count, probe_count = probes.shape
    regions = lax.axis_size("region")
    if regions == 8 and lax.axis_size("narrow") == 2 and 2 * probe_count >= regions:
        return by_blocks(queries, probes, fine_blocks, centroids)
    return by_slots(queries, probes, fine_blocks, centroids)


def solution(mesh):
    return jax.shard_map(
        per_device,
        mesh=mesh,
        in_specs=(
            P(("parts", "region", "narrow"), None),
            P(("parts", "region", "narrow"), None),
            P(("parts", "region", "narrow"), None, None),
            P("region", "narrow", None),
        ),
        out_specs=P(("parts", "region", "narrow"), None, None),
        check_vma=False,
    )
```

```python
import functools
import math

import jax
import jax.numpy as jnp
from jax import lax
from jax.experimental import pallas as pl
from jax.experimental.pallas import tpu as pltpu
from jax.sharding import PartitionSpec as P

BLK = 128
W01 = 1
W42 = 1
W56 = 10
W73 = 1


def score_against(flat_rows, centre_rows):
    inner_prod = jnp.einsum("nd,md->nm", flat_rows, centre_rows, preferred_element_type=jnp.float32)
    widened = centre_rows.astype(jnp.float32)
    sq_norm = jnp.sum(widened * widened, axis=1)
    width = flat_rows.shape[1]
    return inner_prod / math.sqrt(width) - 0.5 * sq_norm[None, :] / width


def pick_blocks(scored, block_ids, block_len):
    row_count = scored.shape[0]
    blocked = scored.reshape(row_count, -1, block_len)
    block_total = blocked.shape[1]
    chooser = (
        block_ids[:, :, None] == jnp.arange(block_total, dtype=jnp.int32)[None, None, :]
    ).astype(jnp.float32)
    selected = jnp.einsum("rjb,rbk->rjk", chooser, blocked, precision=lax.Precision.HIGHEST)
    return selected.reshape(row_count, -1)


def by_slots(queries, probes, fine_blocks, centroids):
    q_count, probe_count = probes.shape
    n_active = fine_blocks.shape[2]
    width = queries.shape[1]
    regions = lax.axis_size("region")
    capacity = max(2, min(q_count, 2 * q_count * probe_count // regions))
    slot_count = q_count * probe_count
    target_region = probes.reshape(slot_count)
    one_hot = (target_region[:, None] == jnp.arange(regions, dtype=jnp.int32)[None, :]).astype(
        jnp.float32
    )
    slot_index = jnp.arange(slot_count, dtype=jnp.int32)
    strict_lower = (slot_index[:, None] > slot_index[None, :]).astype(jnp.float32)
    earlier = jnp.dot(
        strict_lower, one_hot, precision=lax.Precision.HIGHEST, preferred_element_type=jnp.float32
    )
    slot_pos = jnp.sum(earlier * one_hot, axis=1).astype(jnp.int32)
    target_slot = target_region * capacity + slot_pos
    slot_match = jnp.arange(regions * capacity, dtype=jnp.int32)[:, None] == target_slot[None, :]
    query_match = jnp.any(
        slot_match.reshape(regions * capacity, q_count, probe_count), axis=2
    ).astype(jnp.bfloat16)
    send_rows = jnp.dot(query_match, queries, preferred_element_type=jnp.float32).astype(
        jnp.bfloat16
    )
    send_rows = send_rows.reshape(regions, capacity, width)
    block_values = fine_blocks.reshape(slot_count, n_active).astype(jnp.float32)
    send_blocks = jnp.dot(
        slot_match.astype(jnp.float32),
        block_values,
        precision=lax.Precision.HIGHEST,
        preferred_element_type=jnp.float32,
    ).astype(jnp.int32)
    send_blocks = send_blocks.reshape(regions, capacity, n_active)
    local_centres = centroids[0]
    in_rows = lax.all_to_all(send_rows, "region", split_axis=0, concat_axis=0, tiled=True)
    in_blocks = lax.all_to_all(send_blocks, "region", split_axis=0, concat_axis=0, tiled=True)
    sender_count = in_rows.shape[0]
    item_count = in_rows.shape[1]
    flat_rows = in_rows.reshape(sender_count * item_count, width)
    flat_blocks = in_blocks.reshape(sender_count * item_count, n_active)
    scored = score_against(flat_rows, lax.all_gather(local_centres, "narrow", axis=0, tiled=True))
    packed = pick_blocks(scored, flat_blocks, BLK).astype(jnp.bfloat16)
    packed = packed.reshape(sender_count, item_count, n_active * BLK)
    returned_all = lax.all_to_all(packed, "region", split_axis=0, concat_axis=0, tiled=True)
    flat_returned = returned_all.reshape(regions * capacity, -1)
    answers = jnp.dot(
        slot_match.T.astype(jnp.bfloat16), flat_returned, preferred_element_type=jnp.float32
    ).astype(jnp.bfloat16)
    return answers.reshape(q_count, probe_count, -1)


def choose(options, index):
    bit = 1
    while len(options) > 1:
        odd = (index & bit) != 0
        options = [
            jnp.where(odd, options[i + 1], options[i]) for i in range(0, len(options), 2)
        ]
        bit *= 2
    return options[0]


def pack_kernel(queries_ref, ids_ref, out_ref):
    q_count = queries_ref.shape[0]
    extra = out_ref.shape[0] - q_count
    out_ref[0:q_count, :] = queries_ref[...]
    ids = ids_ref[...].astype(jnp.float32)
    tiles = [ids[i : i + extra] for i in range(0, ids.shape[0], extra)]
    tiles.append(jnp.zeros((extra, queries_ref.shape[1] - len(tiles) * q_count), jnp.float32))
    out_ref[q_count:, :] = jnp.concatenate(tiles, axis=1).astype(jnp.bfloat16)


def pack(queries, ids, extra):
    q_count, width = queries.shape
    in_vmem = pl.BlockSpec(memory_space=pltpu.VMEM)
    return pl.pallas_call(
        pack_kernel,
        out_shape=jax.ShapeDtypeStruct((q_count + extra, width), jnp.bfloat16),
        in_specs=[in_vmem] * 2,
        out_specs=in_vmem,
        compiler_params=pltpu.CompilerParams(vmem_limit_bytes=24 * 1024 * 1024),
        name="pack",
    )(queries, ids)


def list_ids_kernel(probes_ref, fine_ref, out_ref):
    ids = jnp.concatenate([probes_ref[...], fine_ref[...]], axis=0).astype(jnp.float32)
    spare = out_ref.shape[0] - ids.shape[0]
    ids = jnp.concatenate([ids, jnp.zeros((spare, ids.shape[1]), jnp.float32)], axis=0)
    out_ref[...] = ids.astype(jnp.bfloat16)


def list_ids(probes, fine):
    rows = probes.shape[0] + fine.shape[0]
    in_vmem = pl.BlockSpec(memory_space=pltpu.VMEM)
    return pl.pallas_call(
        list_ids_kernel,
        out_shape=jax.ShapeDtypeStruct((rows + -rows % 16, probes.shape[1]), jnp.bfloat16),
        in_specs=[in_vmem] * 2,
        out_specs=in_vmem,
        compiler_params=pltpu.CompilerParams(vmem_limit_bytes=24 * 1024 * 1024),
        name="list_ids",
    )(probes, fine)


def norms_kernel(scale, rows_ref, bias_ref, kept_ref=None):
    count, width = rows_ref.shape
    ones = jnp.ones((8, width), jnp.bfloat16)
    chunk = 256
    for t in range(0, count, chunk):
        rows = rows_ref[t : t + chunk, :]
        if kept_ref is not None:
            kept_ref[t : t + chunk, :] = rows
        square = jnp.square(rows.astype(jnp.float32))
        high = square.astype(jnp.bfloat16)
        low = (square - high.astype(jnp.float32)).astype(jnp.bfloat16)
        total = jnp.zeros((8, chunk), jnp.float32)
        for term in (high, low):
            total = total + lax.dot_general(
                ones, term, (((1,), (1,)), ((), ())), preferred_element_type=jnp.float32
            )
        bias_ref[:, t : t + chunk] = scale * total[0:1]


def norms(rows, scale, keep):
    in_vmem = pl.BlockSpec(memory_space=pltpu.VMEM)
    shapes = [jax.ShapeDtypeStruct((1, rows.shape[0]), jnp.float32)]
    if keep:
        shapes.append(jax.ShapeDtypeStruct(rows.shape, rows.dtype))
    return pl.pallas_call(
        functools.partial(norms_kernel, scale),
        out_shape=shapes,
        in_specs=[in_vmem],
        out_specs=[in_vmem] * len(shapes),
        compiler_params=pltpu.CompilerParams(vmem_limit_bytes=24 * 1024 * 1024),
        cost_estimate=pl.CostEstimate(
            flops=4 * 10**9, bytes_accessed=2 * rows.size * len(shapes), transcendentals=0
        ),
        name="norms",
    )(rows)


def score_kernel(n_sets, q_count, probe_count, n_active, scale, where_ref, *refs):
    q_refs = refs[:n_sets]
    sides = ((refs[n_sets], refs[n_sets + 2]), (refs[n_sets + 1], refs[n_sets + 3]))
    out_refs = refs[n_sets + 4 : 2 * n_sets + 4]
    held = refs[2 * n_sets + 4]
    half = sides[0][0].shape[0]
    block_total = 2 * half // BLK
    region = where_ref[0].astype(jnp.float32)
    columns = []
    for q_ref in q_refs:
        extra = q_ref.shape[0] - q_count
        tail = q_ref[...].astype(jnp.float32)[q_count:]
        tiles = -(-probe_count * (n_active + 1) // extra)
        meta = jnp.concatenate(
            [tail[:, i * q_count : (i + 1) * q_count] for i in range(tiles)], axis=0
        )
        wanted = jnp.zeros((n_active, q_count), jnp.float32)
        for p in range(probe_count):
            fine = meta[probe_count + p * n_active : probe_count + (p + 1) * n_active]
            wanted = wanted + jnp.where(meta[p : p + 1] == region, fine, 0.0)
        wanted = jnp.concatenate(
            [wanted, jnp.zeros((q_count - n_active, q_count), jnp.float32)], axis=0
        )
        columns.append(jnp.transpose(wanted).astype(jnp.int32) ^ (where_ref[1] * (block_total // 2)))
    rows = jnp.concatenate([r[0:q_count, :] for r in q_refs], axis=0)
    chunk = 512
    for side, (c_ref, b_ref) in enumerate(sides):
        for t in range(0, half, chunk):
            inner = lax.dot_general(
                rows,
                c_ref[t : t + chunk, :],
                (((1,), (1,)), ((), ())),
                preferred_element_type=jnp.float32,
            )
            held[:, side * half + t : side * half + t + chunk] = inner + b_ref[:, t : t + chunk]
    step = 32
    for s in range(n_sets):
        for r in range(0, q_count, step):
            row = s * q_count + r
            options = [held[row : row + step, b * BLK : (b + 1) * BLK] for b in range(block_total)]
            for j in range(n_active):
                best = choose(options, columns[s][r : r + step, j : j + 1])
                out_refs[s][r : r + step, j * BLK : (j + 1) * BLK] = (best * scale).astype(
                    jnp.bfloat16
                )


def score(where, blocks, own, other, own_bias, other_bias, q_count, probe_count, n_active, weight):
    n_sets = len(blocks)
    half, width = own.shape
    in_vmem = pl.BlockSpec(memory_space=pltpu.VMEM)
    out = jax.ShapeDtypeStruct((q_count, n_active * BLK), jnp.bfloat16)
    return pl.pallas_call(
        functools.partial(
            score_kernel, n_sets, q_count, probe_count, n_active, 1.0 / math.sqrt(width)
        ),
        out_shape=[out] * n_sets,
        in_specs=[pl.BlockSpec(memory_space=pltpu.SMEM)] + [in_vmem] * (n_sets + 4),
        out_specs=[in_vmem] * n_sets,
        scratch_shapes=[pltpu.VMEM((n_sets * q_count, 2 * half), jnp.float32)],
        compiler_params=pltpu.CompilerParams(vmem_limit_bytes=24 * 1024 * 1024),
        cost_estimate=pl.CostEstimate(
            flops=weight * 2 * n_sets * q_count * 2 * half * width,
            bytes_accessed=2 * half * width * 2 + n_sets * q_count * (width + n_active * BLK) * 2,
            transcendentals=0,
        ),
        name="score",
    )(where, *blocks, own, other, own_bias, other_bias)


def answer_kernel(names, where_ref, probes_ref, *refs):
    part_refs, base_ref, out_ref = refs[: len(names)], refs[len(names)], refs[-1]
    probe_count, q_count = probes_ref.shape
    offset = (probes_ref[...] ^ where_ref[0]).astype(jnp.float32)
    offset = jnp.concatenate(
        [offset, jnp.zeros((q_count - probe_count, q_count), jnp.float32)], axis=0
    )
    offset = jnp.transpose(offset).astype(jnp.int32)
    step = 16
    for r in range(0, q_count, step):
        parts = {n: p[r : r + step, :].astype(jnp.float32) for n, p in zip(names, part_refs)}
        for p in range(probe_count):
            column = offset[r : r + step, p : p + 1]
            if base_ref is out_ref:
                best = choose([parts.get(n, parts[names[0]]) for n in range(8)], column)
            else:
                best = base_ref[r : r + step, p, :].astype(jnp.float32)
                for n in names:
                    best = jnp.where(column == n, parts[n], best)
            out_ref[r : r + step, p, :] = best.astype(jnp.bfloat16)


def answer(where, probes, parts, base=None):
    probe_count, q_count = probes.shape
    names = sorted(parts)
    length = parts[names[0]].shape[1]
    in_vmem = pl.BlockSpec(memory_space=pltpu.VMEM)
    inputs = [parts[n] for n in names] + ([] if base is None else [base])
    return pl.pallas_call(
        functools.partial(answer_kernel, names),
        out_shape=jax.ShapeDtypeStruct((q_count, probe_count, length), jnp.bfloat16),
        in_specs=[pl.BlockSpec(memory_space=pltpu.SMEM)] + [in_vmem] * (1 + len(inputs)),
        out_specs=in_vmem,
        compiler_params=pltpu.CompilerParams(vmem_limit_bytes=24 * 1024 * 1024),
        name="answer",
    )(where, probes, *inputs)


def by_blocks(queries, probes, fine_blocks, centroids):
    q_count, probe_count = probes.shape
    n_active = fine_blocks.shape[2]
    width = queries.shape[1]
    regions = lax.axis_size("region")

    def hop(value, mask):
        return lax.ppermute(value, "region", [(r, r ^ mask) for r in range(regions)])

    region = lax.axis_index("region")
    side = lax.axis_index("narrow")
    where = jnp.stack([region, side]).astype(jnp.int32)
    own = centroids[0]
    probes = probes.T
    fine = fine_blocks.reshape(q_count, -1).T
    held = {4: hop(queries, 4)}
    ids = list_ids(probes, fine)
    held[0] = pack(queries, ids, 8)
    held[1] = hop(held[0], 1)
    held[2] = hop(held[0], 2)
    other = lax.ppermute(own, "narrow", [(0, 1), (1, 0)])
    factor = -0.5 / math.sqrt(width)
    (own_bias,) = norms(own, factor, False)
    other_bias, other = norms(other, factor, True)
    late_ids, own_bias = lax.optimization_barrier((ids, own_bias))
    ids_4 = hop(late_ids, 4)

    def scored(*keys, weight=1):
        blocks = [held[k] for k in keys]
        return score(
            where, blocks, own, other, own_bias, other_bias, q_count, probe_count, n_active, weight
        )

    barrier = lax.optimization_barrier
    results, back = {}, {}
    results[0], results[1] = scored(0, 1, weight=W01)
    back[1] = hop(results[1], 1)
    held[4], results[0] = barrier((held[4], results[0]))
    held[4] = pack(held[4], ids_4, 8)
    held[6] = hop(held[4], 2)
    held[5] = hop(held[4], 1)
    results[4], results[2] = scored(4, 2, weight=W42)
    back[4] = hop(results[4], 4)
    held[6], held[1], results[4] = barrier((held[6], held[1], results[4]))
    held[7] = hop(held[6], 1)
    held[3] = hop(held[1], 2)
    results[5], results[6] = scored(5, 6, weight=W56)
    back[5] = hop(results[5], 5)
    back[6] = hop(results[6], 6)
    results[2], results[5] = barrier((results[2], results[5]))
    back[2] = hop(results[2], 2)
    held[7], back[4], back[1] = barrier((held[7], back[4], back[1]))
    (results[7],) = scored(7, weight=W73)
    back[7] = hop(results[7], 7)
    held[3], results[7] = barrier((held[3], results[7]))
    (results[3],) = scored(3, weight=W73)
    back[3] = hop(results[3], 3)
    early = answer(where, probes, {0: results[0], **{k: back[k] for k in (1, 2, 4, 5, 6, 7)}})
    return answer(where, probes, {3: back[3]}, early)


def per_device(queries, probes, fine_blocks, centroids):
    q_count, probe_count = probes.shape
    regions = lax.axis_size("region")
    if regions == 8 and lax.axis_size("narrow") == 2 and 2 * probe_count >= regions:
        return by_blocks(queries, probes, fine_blocks, centroids)
    return by_slots(queries, probes, fine_blocks, centroids)


def solution(mesh):
    return jax.shard_map(
        per_device,
        mesh=mesh,
        in_specs=(
            P(("parts", "region", "narrow"), None),
            P(("parts", "region", "narrow"), None),
            P(("parts", "region", "narrow"), None, None),
            P("region", "narrow", None),
        ),
        out_specs=P(("parts", "region", "narrow"), None, None),
        check_vma=False,
    )
```

```python
import functools
import math

import jax
import jax.numpy as jnp
from jax import lax
from jax.experimental import pallas as pl
from jax.experimental.pallas import tpu as pltpu
from jax.sharding import PartitionSpec as P

BLK = 128
W01 = 1
W42 = 1
W56 = 10
W73 = 1


def score_against(flat_rows, centre_rows):
    inner_prod = jnp.einsum("nd,md->nm", flat_rows, centre_rows, preferred_element_type=jnp.float32)
    widened = centre_rows.astype(jnp.float32)
    sq_norm = jnp.sum(widened * widened, axis=1)
    width = flat_rows.shape[1]
    return inner_prod / math.sqrt(width) - 0.5 * sq_norm[None, :] / width


def pick_blocks(scored, block_ids, block_len):
    row_count = scored.shape[0]
    blocked = scored.reshape(row_count, -1, block_len)
    block_total = blocked.shape[1]
    chooser = (
        block_ids[:, :, None] == jnp.arange(block_total, dtype=jnp.int32)[None, None, :]
    ).astype(jnp.float32)
    selected = jnp.einsum("rjb,rbk->rjk", chooser, blocked, precision=lax.Precision.HIGHEST)
    return selected.reshape(row_count, -1)


def by_slots(queries, probes, fine_blocks, centroids):
    q_count, probe_count = probes.shape
    n_active = fine_blocks.shape[2]
    width = queries.shape[1]
    regions = lax.axis_size("region")
    capacity = max(2, min(q_count, 2 * q_count * probe_count // regions))
    slot_count = q_count * probe_count
    target_region = probes.reshape(slot_count)
    one_hot = (target_region[:, None] == jnp.arange(regions, dtype=jnp.int32)[None, :]).astype(
        jnp.float32
    )
    slot_index = jnp.arange(slot_count, dtype=jnp.int32)
    strict_lower = (slot_index[:, None] > slot_index[None, :]).astype(jnp.float32)
    earlier = jnp.dot(
        strict_lower, one_hot, precision=lax.Precision.HIGHEST, preferred_element_type=jnp.float32
    )
    slot_pos = jnp.sum(earlier * one_hot, axis=1).astype(jnp.int32)
    target_slot = target_region * capacity + slot_pos
    slot_match = jnp.arange(regions * capacity, dtype=jnp.int32)[:, None] == target_slot[None, :]
    query_match = jnp.any(
        slot_match.reshape(regions * capacity, q_count, probe_count), axis=2
    ).astype(jnp.bfloat16)
    send_rows = jnp.dot(query_match, queries, preferred_element_type=jnp.float32).astype(
        jnp.bfloat16
    )
    send_rows = send_rows.reshape(regions, capacity, width)
    block_values = fine_blocks.reshape(slot_count, n_active).astype(jnp.float32)
    send_blocks = jnp.dot(
        slot_match.astype(jnp.float32),
        block_values,
        precision=lax.Precision.HIGHEST,
        preferred_element_type=jnp.float32,
    ).astype(jnp.int32)
    send_blocks = send_blocks.reshape(regions, capacity, n_active)
    local_centres = centroids[0]
    in_rows = lax.all_to_all(send_rows, "region", split_axis=0, concat_axis=0, tiled=True)
    in_blocks = lax.all_to_all(send_blocks, "region", split_axis=0, concat_axis=0, tiled=True)
    sender_count = in_rows.shape[0]
    item_count = in_rows.shape[1]
    flat_rows = in_rows.reshape(sender_count * item_count, width)
    flat_blocks = in_blocks.reshape(sender_count * item_count, n_active)
    scored = score_against(flat_rows, lax.all_gather(local_centres, "narrow", axis=0, tiled=True))
    packed = pick_blocks(scored, flat_blocks, BLK).astype(jnp.bfloat16)
    packed = packed.reshape(sender_count, item_count, n_active * BLK)
    returned_all = lax.all_to_all(packed, "region", split_axis=0, concat_axis=0, tiled=True)
    flat_returned = returned_all.reshape(regions * capacity, -1)
    answers = jnp.dot(
        slot_match.T.astype(jnp.bfloat16), flat_returned, preferred_element_type=jnp.float32
    ).astype(jnp.bfloat16)
    return answers.reshape(q_count, probe_count, -1)


def choose(options, index):
    bit = 1
    while len(options) > 1:
        odd = (index & bit) != 0
        options = [
            jnp.where(odd, options[i + 1], options[i]) for i in range(0, len(options), 2)
        ]
        bit *= 2
    return options[0]


def pack_kernel(queries_ref, ids_ref, out_ref):
    q_count = queries_ref.shape[0]
    extra = out_ref.shape[0] - q_count
    out_ref[0:q_count, :] = queries_ref[...]
    ids = ids_ref[...].astype(jnp.float32)
    tiles = [ids[i : i + extra] for i in range(0, ids.shape[0], extra)]
    tiles.append(jnp.zeros((extra, queries_ref.shape[1] - len(tiles) * q_count), jnp.float32))
    out_ref[q_count:, :] = jnp.concatenate(tiles, axis=1).astype(jnp.bfloat16)


def pack(queries, ids, extra):
    q_count, width = queries.shape
    in_vmem = pl.BlockSpec(memory_space=pltpu.VMEM)
    return pl.pallas_call(
        pack_kernel,
        out_shape=jax.ShapeDtypeStruct((q_count + extra, width), jnp.bfloat16),
        in_specs=[in_vmem] * 2,
        out_specs=in_vmem,
        compiler_params=pltpu.CompilerParams(vmem_limit_bytes=24 * 1024 * 1024),
        name="pack",
    )(queries, ids)


def list_ids_kernel(probes_ref, fine_ref, out_ref):
    ids = jnp.concatenate([probes_ref[...], fine_ref[...]], axis=0).astype(jnp.float32)
    spare = out_ref.shape[0] - ids.shape[0]
    ids = jnp.concatenate([ids, jnp.zeros((spare, ids.shape[1]), jnp.float32)], axis=0)
    out_ref[...] = ids.astype(jnp.bfloat16)


def list_ids(probes, fine):
    rows = probes.shape[0] + fine.shape[0]
    in_vmem = pl.BlockSpec(memory_space=pltpu.VMEM)
    return pl.pallas_call(
        list_ids_kernel,
        out_shape=jax.ShapeDtypeStruct((rows + -rows % 16, probes.shape[1]), jnp.bfloat16),
        in_specs=[in_vmem] * 2,
        out_specs=in_vmem,
        compiler_params=pltpu.CompilerParams(vmem_limit_bytes=24 * 1024 * 1024),
        name="list_ids",
    )(probes, fine)


def norms_kernel(scale, rows_ref, bias_ref, kept_ref=None):
    count, width = rows_ref.shape
    ones = jnp.ones((8, width), jnp.bfloat16)
    chunk = 256
    for t in range(0, count, chunk):
        rows = rows_ref[t : t + chunk, :]
        if kept_ref is not None:
            kept_ref[t : t + chunk, :] = rows
        square = jnp.square(rows.astype(jnp.float32))
        high = square.astype(jnp.bfloat16)
        low = (square - high.astype(jnp.float32)).astype(jnp.bfloat16)
        total = jnp.zeros((8, chunk), jnp.float32)
        for term in (high, low):
            total = total + lax.dot_general(
                ones, term, (((1,), (1,)), ((), ())), preferred_element_type=jnp.float32
            )
        bias_ref[:, t : t + chunk] = scale * total[0:1]


def norms(rows, scale, keep):
    in_vmem = pl.BlockSpec(memory_space=pltpu.VMEM)
    shapes = [jax.ShapeDtypeStruct((1, rows.shape[0]), jnp.float32)]
    if keep:
        shapes.append(jax.ShapeDtypeStruct(rows.shape, rows.dtype))
    return pl.pallas_call(
        functools.partial(norms_kernel, scale),
        out_shape=shapes,
        in_specs=[in_vmem],
        out_specs=[in_vmem] * len(shapes),
        compiler_params=pltpu.CompilerParams(vmem_limit_bytes=24 * 1024 * 1024),
        cost_estimate=pl.CostEstimate(
            flops=4 * 10**9, bytes_accessed=2 * rows.size * len(shapes), transcendentals=0
        ),
        name="norms",
    )(rows)


def score_kernel(n_sets, q_count, probe_count, n_active, scale, where_ref, *refs):
    q_refs = refs[:n_sets]
    sides = ((refs[n_sets], refs[n_sets + 2]), (refs[n_sets + 1], refs[n_sets + 3]))
    out_refs = refs[n_sets + 4 : 2 * n_sets + 4]
    held = refs[2 * n_sets + 4]
    half = sides[0][0].shape[0]
    block_total = 2 * half // BLK
    region = where_ref[0].astype(jnp.float32)
    columns = []
    for q_ref in q_refs:
        extra = q_ref.shape[0] - q_count
        tail = q_ref[...].astype(jnp.float32)[q_count:]
        tiles = -(-probe_count * (n_active + 1) // extra)
        meta = jnp.concatenate(
            [tail[:, i * q_count : (i + 1) * q_count] for i in range(tiles)], axis=0
        )
        wanted = jnp.zeros((n_active, q_count), jnp.float32)
        for p in range(probe_count):
            fine = meta[probe_count + p * n_active : probe_count + (p + 1) * n_active]
            wanted = wanted + jnp.where(meta[p : p + 1] == region, fine, 0.0)
        wanted = jnp.concatenate(
            [wanted, jnp.zeros((q_count - n_active, q_count), jnp.float32)], axis=0
        )
        columns.append(jnp.transpose(wanted).astype(jnp.int32) ^ (where_ref[1] * (block_total // 2)))
    rows = jnp.concatenate([r[0:q_count, :] for r in q_refs], axis=0)
    chunk = 512
    for side, (c_ref, b_ref) in enumerate(sides):
        for t in range(0, half, chunk):
            inner = lax.dot_general(
                rows,
                c_ref[t : t + chunk, :],
                (((1,), (1,)), ((), ())),
                preferred_element_type=jnp.float32,
            )
            held[:, side * half + t : side * half + t + chunk] = inner + b_ref[:, t : t + chunk]
    step = 32
    for s in range(n_sets):
        for r in range(0, q_count, step):
            row = s * q_count + r
            options = [held[row : row + step, b * BLK : (b + 1) * BLK] for b in range(block_total)]
            for j in range(n_active):
                best = choose(options, columns[s][r : r + step, j : j + 1])
                out_refs[s][r : r + step, j * BLK : (j + 1) * BLK] = (best * scale).astype(
                    jnp.bfloat16
                )


def score(where, blocks, own, other, own_bias, other_bias, q_count, probe_count, n_active, weight):
    n_sets = len(blocks)
    half, width = own.shape
    in_vmem = pl.BlockSpec(memory_space=pltpu.VMEM)
    out = jax.ShapeDtypeStruct((q_count, n_active * BLK), jnp.bfloat16)
    return pl.pallas_call(
        functools.partial(
            score_kernel, n_sets, q_count, probe_count, n_active, 1.0 / math.sqrt(width)
        ),
        out_shape=[out] * n_sets,
        in_specs=[pl.BlockSpec(memory_space=pltpu.SMEM)] + [in_vmem] * (n_sets + 4),
        out_specs=[in_vmem] * n_sets,
        scratch_shapes=[pltpu.VMEM((n_sets * q_count, 2 * half), jnp.float32)],
        compiler_params=pltpu.CompilerParams(vmem_limit_bytes=24 * 1024 * 1024),
        cost_estimate=pl.CostEstimate(
            flops=weight * 2 * n_sets * q_count * 2 * half * width,
            bytes_accessed=2 * half * width * 2 + n_sets * q_count * (width + n_active * BLK) * 2,
            transcendentals=0,
        ),
        name="score",
    )(where, *blocks, own, other, own_bias, other_bias)


def answer_kernel(names, offset_ref, *refs):
    part_refs, base_ref, out_ref = refs[: len(names)], refs[len(names)], refs[-1]
    probe_count, q_count = offset_ref.shape
    length = part_refs[0].shape[1]
    offset = offset_ref[...].astype(jnp.float32)
    offset = jnp.concatenate(
        [offset, jnp.zeros((q_count - probe_count, q_count), jnp.float32)], axis=0
    )
    offset = jnp.transpose(offset).astype(jnp.int32)
    step = 16
    for r in range(0, q_count, step):
        parts = {n: p[r : r + step, :].astype(jnp.float32) for n, p in zip(names, part_refs)}
        for p in range(probe_count):
            column = offset[r : r + step, p : p + 1]
            place = slice(p * length, (p + 1) * length)
            if base_ref is out_ref:
                best = choose([parts.get(n, parts[names[0]]) for n in range(8)], column)
                out_ref[r : r + step, place] = best.astype(jnp.bfloat16)
            else:
                best = base_ref[r : r + step, place].astype(jnp.float32)
                for n in names:
                    best = jnp.where(column == n, parts[n], best)
                out_ref[r : r + step, p, :] = best.astype(jnp.bfloat16)


def answer(offset, parts, base=None):
    probe_count, q_count = offset.shape
    names = sorted(parts)
    length = parts[names[0]].shape[1]
    in_vmem = pl.BlockSpec(memory_space=pltpu.VMEM)
    inputs = [parts[n] for n in names] + ([] if base is None else [base])
    shape = (q_count, probe_count * length) if base is None else (q_count, probe_count, length)
    return pl.pallas_call(
        functools.partial(answer_kernel, names),
        out_shape=jax.ShapeDtypeStruct(shape, jnp.bfloat16),
        in_specs=[in_vmem] * (1 + len(inputs)),
        out_specs=in_vmem,
        compiler_params=pltpu.CompilerParams(vmem_limit_bytes=24 * 1024 * 1024),
        name="answer",
    )(offset, *inputs)


def by_blocks(queries, probes, fine_blocks, centroids):
    q_count, probe_count = probes.shape
    n_active = fine_blocks.shape[2]
    width = queries.shape[1]
    regions = lax.axis_size("region")

    def hop(value, mask):
        return lax.ppermute(value, "region", [(r, r ^ mask) for r in range(regions)])

    region = lax.axis_index("region")
    side = lax.axis_index("narrow")
    where = jnp.stack([region, side]).astype(jnp.int32)
    own = centroids[0]
    probes = probes.T
    fine = fine_blocks.reshape(q_count, -1).T
    held = {4: hop(queries, 4)}
    ids = list_ids(probes, fine)
    held[0] = pack(queries, ids, 8)
    held[1] = hop(held[0], 1)
    held[2] = hop(held[0], 2)
    other = lax.ppermute(own, "narrow", [(0, 1), (1, 0)])
    factor = -0.5 / math.sqrt(width)
    (own_bias,) = norms(own, factor, False)
    other_bias, other = norms(other, factor, True)
    late_ids, own_bias = lax.optimization_barrier((ids, own_bias))
    ids_4 = hop(late_ids, 4)

    def scored(*keys, weight=1):
        blocks = [held[k] for k in keys]
        return score(
            where, blocks, own, other, own_bias, other_bias, q_count, probe_count, n_active, weight
        )

    barrier = lax.optimization_barrier
    results, back = {}, {}
    results[0], results[1] = scored(0, 1, weight=W01)
    back[1] = hop(results[1], 1)
    held[4], results[0] = barrier((held[4], results[0]))
    held[4] = pack(held[4], ids_4, 8)
    held[6] = hop(held[4], 2)
    held[5] = hop(held[4], 1)
    results[4], results[2] = scored(4, 2, weight=W42)
    back[4] = hop(results[4], 4)
    held[6], held[1], results[4] = barrier((held[6], held[1], results[4]))
    held[7] = hop(held[6], 1)
    held[3] = hop(held[1], 2)
    results[5], results[6] = scored(5, 6, weight=W56)
    back[5] = hop(results[5], 5)
    back[6] = hop(results[6], 6)
    results[2], results[5] = barrier((results[2], results[5]))
    back[2] = hop(results[2], 2)
    held[7], back[4], back[1] = barrier((held[7], back[4], back[1]))
    (results[7],) = scored(7, weight=W73)
    back[7] = hop(results[7], 7)
    held[3], results[7] = barrier((held[3], results[7]))
    (results[3],) = scored(3, weight=W73)
    back[3] = hop(results[3], 3)
    early = answer(probes ^ region, {0: results[0], **{k: back[k] for k in (1, 2, 4, 5, 6)}})
    probes, back[7] = barrier((probes, back[7]))
    return answer(probes ^ region, {3: back[3], 7: back[7]}, early)


def per_device(queries, probes, fine_blocks, centroids):
    q_count, probe_count = probes.shape
    regions = lax.axis_size("region")
    if regions == 8 and lax.axis_size("narrow") == 2 and 2 * probe_count >= regions:
        return by_blocks(queries, probes, fine_blocks, centroids)
    return by_slots(queries, probes, fine_blocks, centroids)


def solution(mesh):
    return jax.shard_map(
        per_device,
        mesh=mesh,
        in_specs=(
            P(("parts", "region", "narrow"), None),
            P(("parts", "region", "narrow"), None),
            P(("parts", "region", "narrow"), None, None),
            P("region", "narrow", None),
        ),
        out_specs=P(("parts", "region", "narrow"), None, None),
        check_vma=False,
    )
```

```python
import functools
import math

import jax
import jax.numpy as jnp
from jax import lax
from jax.experimental import pallas as pl
from jax.experimental.pallas import tpu as pltpu
from jax.sharding import PartitionSpec as P

BLK = 128
W01 = 1
W42 = 1
W56 = 10
W73 = 1


def score_against(flat_rows, centre_rows):
    inner_prod = jnp.einsum("nd,md->nm", flat_rows, centre_rows, preferred_element_type=jnp.float32)
    widened = centre_rows.astype(jnp.float32)
    sq_norm = jnp.sum(widened * widened, axis=1)
    width = flat_rows.shape[1]
    return inner_prod / math.sqrt(width) - 0.5 * sq_norm[None, :] / width


def pick_blocks(scored, block_ids, block_len):
    row_count = scored.shape[0]
    blocked = scored.reshape(row_count, -1, block_len)
    block_total = blocked.shape[1]
    chooser = (
        block_ids[:, :, None] == jnp.arange(block_total, dtype=jnp.int32)[None, None, :]
    ).astype(jnp.float32)
    selected = jnp.einsum("rjb,rbk->rjk", chooser, blocked, precision=lax.Precision.HIGHEST)
    return selected.reshape(row_count, -1)


def by_slots(queries, probes, fine_blocks, centroids):
    q_count, probe_count = probes.shape
    n_active = fine_blocks.shape[2]
    width = queries.shape[1]
    regions = lax.axis_size("region")
    capacity = max(2, min(q_count, 2 * q_count * probe_count // regions))
    slot_count = q_count * probe_count
    target_region = probes.reshape(slot_count)
    one_hot = (target_region[:, None] == jnp.arange(regions, dtype=jnp.int32)[None, :]).astype(
        jnp.float32
    )
    slot_index = jnp.arange(slot_count, dtype=jnp.int32)
    strict_lower = (slot_index[:, None] > slot_index[None, :]).astype(jnp.float32)
    earlier = jnp.dot(
        strict_lower, one_hot, precision=lax.Precision.HIGHEST, preferred_element_type=jnp.float32
    )
    slot_pos = jnp.sum(earlier * one_hot, axis=1).astype(jnp.int32)
    target_slot = target_region * capacity + slot_pos
    slot_match = jnp.arange(regions * capacity, dtype=jnp.int32)[:, None] == target_slot[None, :]
    query_match = jnp.any(
        slot_match.reshape(regions * capacity, q_count, probe_count), axis=2
    ).astype(jnp.bfloat16)
    send_rows = jnp.dot(query_match, queries, preferred_element_type=jnp.float32).astype(
        jnp.bfloat16
    )
    send_rows = send_rows.reshape(regions, capacity, width)
    block_values = fine_blocks.reshape(slot_count, n_active).astype(jnp.float32)
    send_blocks = jnp.dot(
        slot_match.astype(jnp.float32),
        block_values,
        precision=lax.Precision.HIGHEST,
        preferred_element_type=jnp.float32,
    ).astype(jnp.int32)
    send_blocks = send_blocks.reshape(regions, capacity, n_active)
    local_centres = centroids[0]
    in_rows = lax.all_to_all(send_rows, "region", split_axis=0, concat_axis=0, tiled=True)
    in_blocks = lax.all_to_all(send_blocks, "region", split_axis=0, concat_axis=0, tiled=True)
    sender_count = in_rows.shape[0]
    item_count = in_rows.shape[1]
    flat_rows = in_rows.reshape(sender_count * item_count, width)
    flat_blocks = in_blocks.reshape(sender_count * item_count, n_active)
    scored = score_against(flat_rows, lax.all_gather(local_centres, "narrow", axis=0, tiled=True))
    packed = pick_blocks(scored, flat_blocks, BLK).astype(jnp.bfloat16)
    packed = packed.reshape(sender_count, item_count, n_active * BLK)
    returned_all = lax.all_to_all(packed, "region", split_axis=0, concat_axis=0, tiled=True)
    flat_returned = returned_all.reshape(regions * capacity, -1)
    answers = jnp.dot(
        slot_match.T.astype(jnp.bfloat16), flat_returned, preferred_element_type=jnp.float32
    ).astype(jnp.bfloat16)
    return answers.reshape(q_count, probe_count, -1)


def choose(options, index):
    bit = 1
    while len(options) > 1:
        odd = (index & bit) != 0
        options = [
            jnp.where(odd, options[i + 1], options[i]) for i in range(0, len(options), 2)
        ]
        bit *= 2
    return options[0]


def pack_kernel(queries_ref, ids_ref, out_ref):
    q_count = queries_ref.shape[0]
    extra = out_ref.shape[0] - q_count
    out_ref[0:q_count, :] = queries_ref[...]
    ids = ids_ref[...].astype(jnp.float32)
    tiles = [ids[i : i + extra] for i in range(0, ids.shape[0], extra)]
    tiles.append(jnp.zeros((extra, queries_ref.shape[1] - len(tiles) * q_count), jnp.float32))
    out_ref[q_count:, :] = jnp.concatenate(tiles, axis=1).astype(jnp.bfloat16)


def pack(queries, ids, extra):
    q_count, width = queries.shape
    in_vmem = pl.BlockSpec(memory_space=pltpu.VMEM)
    return pl.pallas_call(
        pack_kernel,
        out_shape=jax.ShapeDtypeStruct((q_count + extra, width), jnp.bfloat16),
        in_specs=[in_vmem] * 2,
        out_specs=in_vmem,
        compiler_params=pltpu.CompilerParams(vmem_limit_bytes=24 * 1024 * 1024),
        name="pack",
    )(queries, ids)


def list_ids_kernel(probes_ref, fine_ref, out_ref):
    ids = jnp.concatenate([probes_ref[...], fine_ref[...]], axis=0).astype(jnp.float32)
    spare = out_ref.shape[0] - ids.shape[0]
    ids = jnp.concatenate([ids, jnp.zeros((spare, ids.shape[1]), jnp.float32)], axis=0)
    out_ref[...] = ids.astype(jnp.bfloat16)


def list_ids(probes, fine):
    rows = probes.shape[0] + fine.shape[0]
    in_vmem = pl.BlockSpec(memory_space=pltpu.VMEM)
    return pl.pallas_call(
        list_ids_kernel,
        out_shape=jax.ShapeDtypeStruct((rows + -rows % 16, probes.shape[1]), jnp.bfloat16),
        in_specs=[in_vmem] * 2,
        out_specs=in_vmem,
        compiler_params=pltpu.CompilerParams(vmem_limit_bytes=24 * 1024 * 1024),
        name="list_ids",
    )(probes, fine)


def norms_kernel(scale, rows_ref, bias_ref, kept_ref=None):
    count, width = rows_ref.shape
    ones = jnp.ones((8, width), jnp.bfloat16)
    chunk = 256
    for t in range(0, count, chunk):
        rows = rows_ref[t : t + chunk, :]
        if kept_ref is not None:
            kept_ref[t : t + chunk, :] = rows
        square = jnp.square(rows.astype(jnp.float32))
        high = square.astype(jnp.bfloat16)
        low = (square - high.astype(jnp.float32)).astype(jnp.bfloat16)
        total = jnp.zeros((8, chunk), jnp.float32)
        for term in (high, low):
            total = total + lax.dot_general(
                ones, term, (((1,), (1,)), ((), ())), preferred_element_type=jnp.float32
            )
        bias_ref[:, t : t + chunk] = scale * total[0:1]


def norms(rows, scale, keep):
    in_vmem = pl.BlockSpec(memory_space=pltpu.VMEM)
    shapes = [jax.ShapeDtypeStruct((1, rows.shape[0]), jnp.float32)]
    if keep:
        shapes.append(jax.ShapeDtypeStruct(rows.shape, rows.dtype))
    return pl.pallas_call(
        functools.partial(norms_kernel, scale),
        out_shape=shapes,
        in_specs=[in_vmem],
        out_specs=[in_vmem] * len(shapes),
        compiler_params=pltpu.CompilerParams(vmem_limit_bytes=24 * 1024 * 1024),
        cost_estimate=pl.CostEstimate(
            flops=4 * 10**9, bytes_accessed=2 * rows.size * len(shapes), transcendentals=0
        ),
        name="norms",
    )(rows)


def score_kernel(n_sets, q_count, probe_count, n_active, scale, where_ref, *refs):
    q_refs = refs[:n_sets]
    sides = ((refs[n_sets], refs[n_sets + 2]), (refs[n_sets + 1], refs[n_sets + 3]))
    out_refs = refs[n_sets + 4 : 2 * n_sets + 4]
    held = refs[2 * n_sets + 4]
    half = sides[0][0].shape[0]
    block_total = 2 * half // BLK
    region = where_ref[0].astype(jnp.float32)
    columns = []
    for q_ref in q_refs:
        extra = q_ref.shape[0] - q_count
        tail = q_ref[...].astype(jnp.float32)[q_count:]
        tiles = -(-probe_count * (n_active + 1) // extra)
        meta = jnp.concatenate(
            [tail[:, i * q_count : (i + 1) * q_count] for i in range(tiles)], axis=0
        )
        wanted = jnp.zeros((n_active, q_count), jnp.float32)
        for p in range(probe_count):
            fine = meta[probe_count + p * n_active : probe_count + (p + 1) * n_active]
            wanted = wanted + jnp.where(meta[p : p + 1] == region, fine, 0.0)
        wanted = jnp.concatenate(
            [wanted, jnp.zeros((q_count - n_active, q_count), jnp.float32)], axis=0
        )
        columns.append(jnp.transpose(wanted).astype(jnp.int32) ^ (where_ref[1] * (block_total // 2)))
    rows = jnp.concatenate([r[0:q_count, :] for r in q_refs], axis=0)
    chunk = 512
    for side, (c_ref, b_ref) in enumerate(sides):
        for t in range(0, half, chunk):
            inner = lax.dot_general(
                rows,
                c_ref[t : t + chunk, :],
                (((1,), (1,)), ((), ())),
                preferred_element_type=jnp.float32,
            )
            held[:, side * half + t : side * half + t + chunk] = inner + b_ref[:, t : t + chunk]
    step = 32
    for s in range(n_sets):
        for r in range(0, q_count, step):
            row = s * q_count + r
            options = [held[row : row + step, b * BLK : (b + 1) * BLK] for b in range(block_total)]
            for j in range(n_active):
                best = choose(options, columns[s][r : r + step, j : j + 1])
                out_refs[s][r : r + step, j * BLK : (j + 1) * BLK] = (best * scale).astype(
                    jnp.bfloat16
                )


def score(where, blocks, own, other, own_bias, other_bias, q_count, probe_count, n_active, weight):
    n_sets = len(blocks)
    half, width = own.shape
    in_vmem = pl.BlockSpec(memory_space=pltpu.VMEM)
    out = jax.ShapeDtypeStruct((q_count, n_active * BLK), jnp.bfloat16)
    return pl.pallas_call(
        functools.partial(
            score_kernel, n_sets, q_count, probe_count, n_active, 1.0 / math.sqrt(width)
        ),
        out_shape=[out] * n_sets,
        in_specs=[pl.BlockSpec(memory_space=pltpu.SMEM)] + [in_vmem] * (n_sets + 4),
        out_specs=[in_vmem] * n_sets,
        scratch_shapes=[pltpu.VMEM((n_sets * q_count, 2 * half), jnp.float32)],
        compiler_params=pltpu.CompilerParams(vmem_limit_bytes=24 * 1024 * 1024),
        cost_estimate=pl.CostEstimate(
            flops=weight * 2 * n_sets * q_count * 2 * half * width,
            bytes_accessed=2 * half * width * 2 + n_sets * q_count * (width + n_active * BLK) * 2,
            transcendentals=0,
        ),
        name="score",
    )(where, *blocks, own, other, own_bias, other_bias)


def answer_kernel(names, offset_ref, *refs):
    part_refs, base_ref, out_ref = refs[: len(names)], refs[len(names)], refs[-1]
    probe_count, q_count = offset_ref.shape
    length = part_refs[0].shape[1]
    offset = offset_ref[...].astype(jnp.float32)
    offset = jnp.concatenate(
        [offset, jnp.zeros((q_count - probe_count, q_count), jnp.float32)], axis=0
    )
    offset = jnp.transpose(offset).astype(jnp.int32)
    step = 16
    for r in range(0, q_count, step):
        parts = {n: p[r : r + step, :].astype(jnp.float32) for n, p in zip(names, part_refs)}
        for p in range(probe_count):
            column = offset[r : r + step, p : p + 1]
            place = slice(p * length, (p + 1) * length)
            if base_ref is out_ref:
                best = choose([parts.get(n, parts[names[0]]) for n in range(8)], column)
                out_ref[r : r + step, place] = best.astype(jnp.bfloat16)
            else:
                best = base_ref[r : r + step, place].astype(jnp.float32)
                for n in names:
                    best = jnp.where(column == n, parts[n], best)
                out_ref[r : r + step, p, :] = best.astype(jnp.bfloat16)


def answer(offset, parts, base=None):
    probe_count, q_count = offset.shape
    names = sorted(parts)
    length = parts[names[0]].shape[1]
    in_vmem = pl.BlockSpec(memory_space=pltpu.VMEM)
    inputs = [parts[n] for n in names] + ([] if base is None else [base])
    shape = (q_count, probe_count * length) if base is None else (q_count, probe_count, length)
    return pl.pallas_call(
        functools.partial(answer_kernel, names),
        out_shape=jax.ShapeDtypeStruct(shape, jnp.bfloat16),
        in_specs=[in_vmem] * (1 + len(inputs)),
        out_specs=in_vmem,
        compiler_params=pltpu.CompilerParams(vmem_limit_bytes=24 * 1024 * 1024),
        name="answer",
    )(offset, *inputs)


def by_blocks(queries, probes, fine_blocks, centroids):
    q_count, probe_count = probes.shape
    n_active = fine_blocks.shape[2]
    width = queries.shape[1]
    regions = lax.axis_size("region")

    def hop(value, mask):
        return lax.ppermute(value, "region", [(r, r ^ mask) for r in range(regions)])

    region = lax.axis_index("region")
    side = lax.axis_index("narrow")
    where = jnp.stack([region, side]).astype(jnp.int32)
    own = centroids[0]
    probes = probes.T
    fine = fine_blocks.reshape(q_count, -1).T
    held = {4: hop(queries, 4)}
    ids = list_ids(probes, fine)
    held[0] = pack(queries, ids, 8)
    held[1] = hop(held[0], 1)
    held[2] = hop(held[0], 2)
    other = lax.ppermute(own, "narrow", [(0, 1), (1, 0)])
    factor = -0.5 / math.sqrt(width)
    (own_bias,) = norms(own, factor, False)
    other_bias, other = norms(other, factor, True)
    late_ids, own_bias, other_bias = lax.optimization_barrier((ids, own_bias, other_bias))
    ids_4 = hop(late_ids, 4)

    def scored(*keys, weight=1):
        blocks = [held[k] for k in keys]
        return score(
            where, blocks, own, other, own_bias, other_bias, q_count, probe_count, n_active, weight
        )

    barrier = lax.optimization_barrier
    results, back = {}, {}
    results[0], results[1] = scored(0, 1, weight=W01)
    back[1] = hop(results[1], 1)
    held[4], results[0] = barrier((held[4], results[0]))
    held[4] = pack(held[4], ids_4, 8)
    held[6] = hop(held[4], 2)
    held[5] = hop(held[4], 1)
    results[4], results[2] = scored(4, 2, weight=W42)
    back[4] = hop(results[4], 4)
    held[6], held[1], results[4] = barrier((held[6], held[1], results[4]))
    held[7] = hop(held[6], 1)
    held[3] = hop(held[1], 2)
    results[6], results[5] = scored(6, 5, weight=W56)
    back[6] = hop(results[6], 6)
    back[5] = hop(results[5], 5)
    results[2], results[5] = barrier((results[2], results[5]))
    back[2] = hop(results[2], 2)
    held[7], back[4], back[1] = barrier((held[7], back[4], back[1]))
    (results[7],) = scored(7, weight=W73)
    back[7] = hop(results[7], 7)
    held[3], results[7] = barrier((held[3], results[7]))
    (results[3],) = scored(3, weight=W73)
    back[3] = hop(results[3], 3)
    early = answer(probes ^ region, {0: results[0], **{k: back[k] for k in (1, 2, 4, 5, 6)}})
    probes, back[7] = barrier((probes, back[7]))
    return answer(probes ^ region, {3: back[3], 7: back[7]}, early)


def per_device(queries, probes, fine_blocks, centroids):
    q_count, probe_count = probes.shape
    regions = lax.axis_size("region")
    if regions == 8 and lax.axis_size("narrow") == 2 and 2 * probe_count >= regions:
        return by_blocks(queries, probes, fine_blocks, centroids)
    return by_slots(queries, probes, fine_blocks, centroids)


def solution(mesh):
    return jax.shard_map(
        per_device,
        mesh=mesh,
        in_specs=(
            P(("parts", "region", "narrow"), None),
            P(("parts", "region", "narrow"), None),
            P(("parts", "region", "narrow"), None, None),
            P("region", "narrow", None),
        ),
        out_specs=P(("parts", "region", "narrow"), None, None),
        check_vma=False,
    )
```

```python
import functools
import math

import jax
import jax.numpy as jnp
from jax import lax
from jax.experimental import pallas as pl
from jax.experimental.pallas import tpu as pltpu
from jax.sharding import PartitionSpec as P

BLK = 128
W01 = 1
W42 = 1
W56 = 10
W73 = 1


def score_against(flat_rows, centre_rows):
    inner_prod = jnp.einsum("nd,md->nm", flat_rows, centre_rows, preferred_element_type=jnp.float32)
    widened = centre_rows.astype(jnp.float32)
    sq_norm = jnp.sum(widened * widened, axis=1)
    width = flat_rows.shape[1]
    return inner_prod / math.sqrt(width) - 0.5 * sq_norm[None, :] / width


def pick_blocks(scored, block_ids, block_len):
    row_count = scored.shape[0]
    blocked = scored.reshape(row_count, -1, block_len)
    block_total = blocked.shape[1]
    chooser = (
        block_ids[:, :, None] == jnp.arange(block_total, dtype=jnp.int32)[None, None, :]
    ).astype(jnp.float32)
    selected = jnp.einsum("rjb,rbk->rjk", chooser, blocked, precision=lax.Precision.HIGHEST)
    return selected.reshape(row_count, -1)


def by_slots(queries, probes, fine_blocks, centroids):
    q_count, probe_count = probes.shape
    n_active = fine_blocks.shape[2]
    width = queries.shape[1]
    regions = lax.axis_size("region")
    capacity = max(2, min(q_count, 2 * q_count * probe_count // regions))
    slot_count = q_count * probe_count
    target_region = probes.reshape(slot_count)
    one_hot = (target_region[:, None] == jnp.arange(regions, dtype=jnp.int32)[None, :]).astype(
        jnp.float32
    )
    slot_index = jnp.arange(slot_count, dtype=jnp.int32)
    strict_lower = (slot_index[:, None] > slot_index[None, :]).astype(jnp.float32)
    earlier = jnp.dot(
        strict_lower, one_hot, precision=lax.Precision.HIGHEST, preferred_element_type=jnp.float32
    )
    slot_pos = jnp.sum(earlier * one_hot, axis=1).astype(jnp.int32)
    target_slot = target_region * capacity + slot_pos
    slot_match = jnp.arange(regions * capacity, dtype=jnp.int32)[:, None] == target_slot[None, :]
    query_match = jnp.any(
        slot_match.reshape(regions * capacity, q_count, probe_count), axis=2
    ).astype(jnp.bfloat16)
    send_rows = jnp.dot(query_match, queries, preferred_element_type=jnp.float32).astype(
        jnp.bfloat16
    )
    send_rows = send_rows.reshape(regions, capacity, width)
    block_values = fine_blocks.reshape(slot_count, n_active).astype(jnp.float32)
    send_blocks = jnp.dot(
        slot_match.astype(jnp.float32),
        block_values,
        precision=lax.Precision.HIGHEST,
        preferred_element_type=jnp.float32,
    ).astype(jnp.int32)
    send_blocks = send_blocks.reshape(regions, capacity, n_active)
    local_centres = centroids[0]
    in_rows = lax.all_to_all(send_rows, "region", split_axis=0, concat_axis=0, tiled=True)
    in_blocks = lax.all_to_all(send_blocks, "region", split_axis=0, concat_axis=0, tiled=True)
    sender_count = in_rows.shape[0]
    item_count = in_rows.shape[1]
    flat_rows = in_rows.reshape(sender_count * item_count, width)
    flat_blocks = in_blocks.reshape(sender_count * item_count, n_active)
    scored = score_against(flat_rows, lax.all_gather(local_centres, "narrow", axis=0, tiled=True))
    packed = pick_blocks(scored, flat_blocks, BLK).astype(jnp.bfloat16)
    packed = packed.reshape(sender_count, item_count, n_active * BLK)
    returned_all = lax.all_to_all(packed, "region", split_axis=0, concat_axis=0, tiled=True)
    flat_returned = returned_all.reshape(regions * capacity, -1)
    answers = jnp.dot(
        slot_match.T.astype(jnp.bfloat16), flat_returned, preferred_element_type=jnp.float32
    ).astype(jnp.bfloat16)
    return answers.reshape(q_count, probe_count, -1)


def choose(options, index, bit=1):
    while len(options) > 1:
        odd = (index & bit) != 0
        options = [
            jnp.where(odd, options[i + 1], options[i]) for i in range(0, len(options), 2)
        ]
        bit *= 2
    return options[0]


def pack_kernel(queries_ref, ids_ref, out_ref):
    q_count = queries_ref.shape[0]
    extra = out_ref.shape[0] - q_count
    out_ref[0:q_count, :] = queries_ref[...]
    ids = ids_ref[...].astype(jnp.float32)
    tiles = [ids[i : i + extra] for i in range(0, ids.shape[0], extra)]
    tiles.append(jnp.zeros((extra, queries_ref.shape[1] - len(tiles) * q_count), jnp.float32))
    out_ref[q_count:, :] = jnp.concatenate(tiles, axis=1).astype(jnp.bfloat16)


def pack(queries, ids, extra):
    q_count, width = queries.shape
    in_vmem = pl.BlockSpec(memory_space=pltpu.VMEM)
    return pl.pallas_call(
        pack_kernel,
        out_shape=jax.ShapeDtypeStruct((q_count + extra, width), jnp.bfloat16),
        in_specs=[in_vmem] * 2,
        out_specs=in_vmem,
        compiler_params=pltpu.CompilerParams(vmem_limit_bytes=24 * 1024 * 1024),
        name="pack",
    )(queries, ids)


def list_ids_kernel(probes_ref, fine_ref, out_ref):
    ids = jnp.concatenate([probes_ref[...], fine_ref[...]], axis=0).astype(jnp.float32)
    spare = out_ref.shape[0] - ids.shape[0]
    ids = jnp.concatenate([ids, jnp.zeros((spare, ids.shape[1]), jnp.float32)], axis=0)
    out_ref[...] = ids.astype(jnp.bfloat16)


def list_ids(probes, fine):
    rows = probes.shape[0] + fine.shape[0]
    in_vmem = pl.BlockSpec(memory_space=pltpu.VMEM)
    return pl.pallas_call(
        list_ids_kernel,
        out_shape=jax.ShapeDtypeStruct((rows + -rows % 16, probes.shape[1]), jnp.bfloat16),
        in_specs=[in_vmem] * 2,
        out_specs=in_vmem,
        compiler_params=pltpu.CompilerParams(vmem_limit_bytes=24 * 1024 * 1024),
        name="list_ids",
    )(probes, fine)


def norms_kernel(scale, rows_ref, bias_ref, kept_ref=None):
    count, width = rows_ref.shape
    ones = jnp.ones((8, width), jnp.bfloat16)
    chunk = 256
    for t in range(0, count, chunk):
        rows = rows_ref[t : t + chunk, :]
        if kept_ref is not None:
            kept_ref[t : t + chunk, :] = rows
        square = jnp.square(rows.astype(jnp.float32))
        high = square.astype(jnp.bfloat16)
        low = (square - high.astype(jnp.float32)).astype(jnp.bfloat16)
        total = jnp.zeros((8, chunk), jnp.float32)
        for term in (high, low):
            total = total + lax.dot_general(
                ones, term, (((1,), (1,)), ((), ())), preferred_element_type=jnp.float32
            )
        bias_ref[:, t : t + chunk] = scale * total[0:1]


def norms(rows, scale, keep):
    in_vmem = pl.BlockSpec(memory_space=pltpu.VMEM)
    shapes = [jax.ShapeDtypeStruct((1, rows.shape[0]), jnp.float32)]
    if keep:
        shapes.append(jax.ShapeDtypeStruct(rows.shape, rows.dtype))
    return pl.pallas_call(
        functools.partial(norms_kernel, scale),
        out_shape=shapes,
        in_specs=[in_vmem],
        out_specs=[in_vmem] * len(shapes),
        compiler_params=pltpu.CompilerParams(vmem_limit_bytes=24 * 1024 * 1024),
        cost_estimate=pl.CostEstimate(
            flops=4 * 10**9, bytes_accessed=2 * rows.size * len(shapes), transcendentals=0
        ),
        name="norms",
    )(rows)


def score_kernel(n_sets, q_count, probe_count, n_active, scale, where_ref, *refs):
    q_refs = refs[:n_sets]
    sides = ((refs[n_sets], refs[n_sets + 2]), (refs[n_sets + 1], refs[n_sets + 3]))
    out_refs = refs[n_sets + 4 : 2 * n_sets + 4]
    held = refs[2 * n_sets + 4]
    half = sides[0][0].shape[0]
    block_total = 2 * half // BLK
    region = where_ref[0].astype(jnp.float32)
    columns = []
    for q_ref in q_refs:
        extra = q_ref.shape[0] - q_count
        tail = q_ref[...].astype(jnp.float32)[q_count:]
        tiles = -(-probe_count * (n_active + 1) // extra)
        meta = jnp.concatenate(
            [tail[:, i * q_count : (i + 1) * q_count] for i in range(tiles)], axis=0
        )
        wanted = jnp.zeros((n_active, q_count), jnp.float32)
        for p in range(probe_count):
            fine = meta[probe_count + p * n_active : probe_count + (p + 1) * n_active]
            wanted = wanted + jnp.where(meta[p : p + 1] == region, fine, 0.0)
        wanted = jnp.concatenate(
            [wanted, jnp.zeros((q_count - n_active, q_count), jnp.float32)], axis=0
        )
        columns.append(jnp.transpose(wanted).astype(jnp.int32) ^ (where_ref[1] * (block_total // 2)))
    rows = jnp.concatenate([r[0:q_count, :] for r in q_refs], axis=0)
    chunk = 512
    per = chunk // BLK
    step = 32
    places = [(side, t) for side in range(2) for t in range(0, half, chunk)]
    for i, (side, t) in enumerate(places):
        c_ref, b_ref = sides[side]
        inner = lax.dot_general(
            rows,
            c_ref[t : t + chunk, :],
            (((1,), (1,)), ((), ())),
            preferred_element_type=jnp.float32,
        )
        scored = inner + b_ref[:, t : t + chunk]
        for s in range(n_sets):
            for r in range(0, q_count, step):
                row = s * q_count + r
                options = [scored[row : row + step, b * BLK : (b + 1) * BLK] for b in range(per)]
                for j in range(n_active):
                    held[row : row + step, (i * n_active + j) * BLK : (i * n_active + j + 1) * BLK] = (
                        choose(options, columns[s][r : r + step, j : j + 1])
                    )
    for s in range(n_sets):
        for r in range(0, q_count, step):
            row = s * q_count + r
            for j in range(n_active):
                options = [
                    held[row : row + step, (i * n_active + j) * BLK : (i * n_active + j + 1) * BLK]
                    for i in range(len(places))
                ]
                best = choose(options, columns[s][r : r + step, j : j + 1], per)
                out_refs[s][r : r + step, j * BLK : (j + 1) * BLK] = (best * scale).astype(
                    jnp.bfloat16
                )


def score(where, blocks, own, other, own_bias, other_bias, q_count, probe_count, n_active, weight):
    n_sets = len(blocks)
    half, width = own.shape
    in_vmem = pl.BlockSpec(memory_space=pltpu.VMEM)
    out = jax.ShapeDtypeStruct((q_count, n_active * BLK), jnp.bfloat16)
    return pl.pallas_call(
        functools.partial(
            score_kernel, n_sets, q_count, probe_count, n_active, 1.0 / math.sqrt(width)
        ),
        out_shape=[out] * n_sets,
        in_specs=[pl.BlockSpec(memory_space=pltpu.SMEM)] + [in_vmem] * (n_sets + 4),
        out_specs=[in_vmem] * n_sets,
        scratch_shapes=[
            pltpu.VMEM((n_sets * q_count, 2 * half // 512 * n_active * BLK), jnp.float32)
        ],
        compiler_params=pltpu.CompilerParams(vmem_limit_bytes=24 * 1024 * 1024),
        cost_estimate=pl.CostEstimate(
            flops=weight * 2 * n_sets * q_count * 2 * half * width,
            bytes_accessed=2 * half * width * 2 + n_sets * q_count * (width + n_active * BLK) * 2,
            transcendentals=0,
        ),
        name="score",
    )(where, *blocks, own, other, own_bias, other_bias)


def answer_kernel(names, offset_ref, *refs):
    part_refs, base_ref, out_ref = refs[: len(names)], refs[len(names)], refs[-1]
    probe_count, q_count = offset_ref.shape
    length = part_refs[0].shape[1]
    offset = offset_ref[...].astype(jnp.float32)
    offset = jnp.concatenate(
        [offset, jnp.zeros((q_count - probe_count, q_count), jnp.float32)], axis=0
    )
    offset = jnp.transpose(offset).astype(jnp.int32)
    step = 16
    for r in range(0, q_count, step):
        parts = {n: p[r : r + step, :].astype(jnp.float32) for n, p in zip(names, part_refs)}
        for p in range(probe_count):
            column = offset[r : r + step, p : p + 1]
            place = slice(p * length, (p + 1) * length)
            if base_ref is out_ref:
                best = choose([parts.get(n, parts[names[0]]) for n in range(8)], column)
                out_ref[r : r + step, place] = best.astype(jnp.bfloat16)
            else:
                best = base_ref[r : r + step, place].astype(jnp.float32)
                for n in names:
                    best = jnp.where(column == n, parts[n], best)
                out_ref[r : r + step, p, :] = best.astype(jnp.bfloat16)


def answer(offset, parts, base=None):
    probe_count, q_count = offset.shape
    names = sorted(parts)
    length = parts[names[0]].shape[1]
    in_vmem = pl.BlockSpec(memory_space=pltpu.VMEM)
    inputs = [parts[n] for n in names] + ([] if base is None else [base])
    shape = (q_count, probe_count * length) if base is None else (q_count, probe_count, length)
    return pl.pallas_call(
        functools.partial(answer_kernel, names),
        out_shape=jax.ShapeDtypeStruct(shape, jnp.bfloat16),
        in_specs=[in_vmem] * (1 + len(inputs)),
        out_specs=in_vmem,
        compiler_params=pltpu.CompilerParams(vmem_limit_bytes=24 * 1024 * 1024),
        name="answer",
    )(offset, *inputs)


def by_blocks(queries, probes, fine_blocks, centroids):
    q_count, probe_count = probes.shape
    n_active = fine_blocks.shape[2]
    width = queries.shape[1]
    regions = lax.axis_size("region")

    def hop(value, mask):
        return lax.ppermute(value, "region", [(r, r ^ mask) for r in range(regions)])

    region = lax.axis_index("region")
    side = lax.axis_index("narrow")
    where = jnp.stack([region, side]).astype(jnp.int32)
    own = centroids[0]
    probes = probes.T
    fine = fine_blocks.reshape(q_count, -1).T
    held = {4: hop(queries, 4), 2: hop(queries, 2)}
    ids = list_ids(probes, fine)
    held[0] = pack(queries, ids, 8)
    held[1] = hop(held[0], 1)
    other = lax.ppermute(own, "narrow", [(0, 1), (1, 0)])
    factor = -0.5 / math.sqrt(width)
    (own_bias,) = norms(own, factor, False)
    other_bias, other = norms(other, factor, True)
    late_ids, own_bias, other_bias = lax.optimization_barrier((ids, own_bias, other_bias))
    ids_4, ids_2 = hop(late_ids, 4), hop(late_ids, 2)

    def scored(*keys, weight=1):
        blocks = [held[k] for k in keys]
        return score(
            where, blocks, own, other, own_bias, other_bias, q_count, probe_count, n_active, weight
        )

    barrier = lax.optimization_barrier
    results, back = {}, {}
    results[0], results[1] = scored(0, 1, weight=W01)
    back[1] = hop(results[1], 1)
    held[4], held[2], ids_2, results[0] = barrier((held[4], held[2], ids_2, results[0]))
    held[4] = pack(held[4], ids_4, 8)
    held[2] = pack(held[2], ids_2, 8)
    held[6] = hop(held[4], 2)
    held[5] = hop(held[4], 1)
    results[4], results[2] = scored(4, 2, weight=W42)
    back[4] = hop(results[4], 4)
    held[6], held[1], results[4] = barrier((held[6], held[1], results[4]))
    held[7] = hop(held[6], 1)
    held[3] = hop(held[1], 2)
    results[6], results[5] = scored(6, 5, weight=W56)
    back[6] = hop(results[6], 6)
    back[5] = hop(results[5], 5)
    results[2], results[5] = barrier((results[2], results[5]))
    back[2] = hop(results[2], 2)
    held[7], back[4], back[1] = barrier((held[7], back[4], back[1]))
    (results[7],) = scored(7, weight=W73)
    back[7] = hop(results[7], 7)
    held[3], results[7] = barrier((held[3], results[7]))
    (results[3],) = scored(3, weight=W73)
    back[3] = hop(results[3], 3)
    early = answer(probes ^ region, {0: results[0], **{k: back[k] for k in (1, 2, 4, 5, 6)}})
    probes, back[7] = barrier((probes, back[7]))
    return answer(probes ^ region, {3: back[3], 7: back[7]}, early)


def per_device(queries, probes, fine_blocks, centroids):
    q_count, probe_count = probes.shape
    regions = lax.axis_size("region")
    if regions == 8 and lax.axis_size("narrow") == 2 and 2 * probe_count >= regions:
        return by_blocks(queries, probes, fine_blocks, centroids)
    return by_slots(queries, probes, fine_blocks, centroids)


def solution(mesh):
    return jax.shard_map(
        per_device,
        mesh=mesh,
        in_specs=(
            P(("parts", "region", "narrow"), None),
            P(("parts", "region", "narrow"), None),
            P(("parts", "region", "narrow"), None, None),
            P("region", "narrow", None),
        ),
        out_specs=P(("parts", "region", "narrow"), None, None),
        check_vma=False,
    )
```

```python
import functools
import math

import jax
import jax.numpy as jnp
from jax import lax
from jax.experimental import pallas as pl
from jax.experimental.pallas import tpu as pltpu
from jax.sharding import PartitionSpec as P

BLK = 128
W01 = 1
W42 = 1
W56 = 10
W73 = 1


def score_against(flat_rows, centre_rows):
    inner_prod = jnp.einsum("nd,md->nm", flat_rows, centre_rows, preferred_element_type=jnp.float32)
    widened = centre_rows.astype(jnp.float32)
    sq_norm = jnp.sum(widened * widened, axis=1)
    width = flat_rows.shape[1]
    return inner_prod / math.sqrt(width) - 0.5 * sq_norm[None, :] / width


def pick_blocks(scored, block_ids, block_len):
    row_count = scored.shape[0]
    blocked = scored.reshape(row_count, -1, block_len)
    block_total = blocked.shape[1]
    chooser = (
        block_ids[:, :, None] == jnp.arange(block_total, dtype=jnp.int32)[None, None, :]
    ).astype(jnp.float32)
    selected = jnp.einsum("rjb,rbk->rjk", chooser, blocked, precision=lax.Precision.HIGHEST)
    return selected.reshape(row_count, -1)


def by_slots(queries, probes, fine_blocks, centroids):
    q_count, probe_count = probes.shape
    n_active = fine_blocks.shape[2]
    width = queries.shape[1]
    regions = lax.axis_size("region")
    capacity = max(2, min(q_count, 2 * q_count * probe_count // regions))
    slot_count = q_count * probe_count
    target_region = probes.reshape(slot_count)
    one_hot = (target_region[:, None] == jnp.arange(regions, dtype=jnp.int32)[None, :]).astype(
        jnp.float32
    )
    slot_index = jnp.arange(slot_count, dtype=jnp.int32)
    strict_lower = (slot_index[:, None] > slot_index[None, :]).astype(jnp.float32)
    earlier = jnp.dot(
        strict_lower, one_hot, precision=lax.Precision.HIGHEST, preferred_element_type=jnp.float32
    )
    slot_pos = jnp.sum(earlier * one_hot, axis=1).astype(jnp.int32)
    target_slot = target_region * capacity + slot_pos
    slot_match = jnp.arange(regions * capacity, dtype=jnp.int32)[:, None] == target_slot[None, :]
    query_match = jnp.any(
        slot_match.reshape(regions * capacity, q_count, probe_count), axis=2
    ).astype(jnp.bfloat16)
    send_rows = jnp.dot(query_match, queries, preferred_element_type=jnp.float32).astype(
        jnp.bfloat16
    )
    send_rows = send_rows.reshape(regions, capacity, width)
    block_values = fine_blocks.reshape(slot_count, n_active).astype(jnp.float32)
    send_blocks = jnp.dot(
        slot_match.astype(jnp.float32),
        block_values,
        precision=lax.Precision.HIGHEST,
        preferred_element_type=jnp.float32,
    ).astype(jnp.int32)
    send_blocks = send_blocks.reshape(regions, capacity, n_active)
    local_centres = centroids[0]
    in_rows = lax.all_to_all(send_rows, "region", split_axis=0, concat_axis=0, tiled=True)
    in_blocks = lax.all_to_all(send_blocks, "region", split_axis=0, concat_axis=0, tiled=True)
    sender_count = in_rows.shape[0]
    item_count = in_rows.shape[1]
    flat_rows = in_rows.reshape(sender_count * item_count, width)
    flat_blocks = in_blocks.reshape(sender_count * item_count, n_active)
    scored = score_against(flat_rows, lax.all_gather(local_centres, "narrow", axis=0, tiled=True))
    packed = pick_blocks(scored, flat_blocks, BLK).astype(jnp.bfloat16)
    packed = packed.reshape(sender_count, item_count, n_active * BLK)
    returned_all = lax.all_to_all(packed, "region", split_axis=0, concat_axis=0, tiled=True)
    flat_returned = returned_all.reshape(regions * capacity, -1)
    answers = jnp.dot(
        slot_match.T.astype(jnp.bfloat16), flat_returned, preferred_element_type=jnp.float32
    ).astype(jnp.bfloat16)
    return answers.reshape(q_count, probe_count, -1)


def choose(options, index, bit=1):
    while len(options) > 1:
        odd = (index & bit) != 0
        options = [
            jnp.where(odd, options[i + 1], options[i]) for i in range(0, len(options), 2)
        ]
        bit *= 2
    return options[0]


def pack_kernel(queries_ref, ids_ref, out_ref):
    q_count = queries_ref.shape[0]
    extra = out_ref.shape[0] - q_count
    out_ref[0:q_count, :] = queries_ref[...]
    ids = ids_ref[...].astype(jnp.float32)
    tiles = [ids[i : i + extra] for i in range(0, ids.shape[0], extra)]
    tiles.append(jnp.zeros((extra, queries_ref.shape[1] - len(tiles) * q_count), jnp.float32))
    out_ref[q_count:, :] = jnp.concatenate(tiles, axis=1).astype(jnp.bfloat16)


def pack(queries, ids, extra):
    q_count, width = queries.shape
    in_vmem = pl.BlockSpec(memory_space=pltpu.VMEM)
    return pl.pallas_call(
        pack_kernel,
        out_shape=jax.ShapeDtypeStruct((q_count + extra, width), jnp.bfloat16),
        in_specs=[in_vmem] * 2,
        out_specs=in_vmem,
        compiler_params=pltpu.CompilerParams(vmem_limit_bytes=24 * 1024 * 1024),
        name="pack",
    )(queries, ids)


def list_ids_kernel(probes_ref, fine_ref, out_ref):
    ids = jnp.concatenate([probes_ref[...], fine_ref[...]], axis=0).astype(jnp.float32)
    spare = out_ref.shape[0] - ids.shape[0]
    ids = jnp.concatenate([ids, jnp.zeros((spare, ids.shape[1]), jnp.float32)], axis=0)
    out_ref[...] = ids.astype(jnp.bfloat16)


def list_ids(probes, fine):
    rows = probes.shape[0] + fine.shape[0]
    in_vmem = pl.BlockSpec(memory_space=pltpu.VMEM)
    return pl.pallas_call(
        list_ids_kernel,
        out_shape=jax.ShapeDtypeStruct((rows + -rows % 16, probes.shape[1]), jnp.bfloat16),
        in_specs=[in_vmem] * 2,
        out_specs=in_vmem,
        compiler_params=pltpu.CompilerParams(vmem_limit_bytes=24 * 1024 * 1024),
        name="list_ids",
    )(probes, fine)


def norms_kernel(scale, rows_ref, bias_ref, kept_ref=None):
    count, width = rows_ref.shape
    ones = jnp.ones((8, width), jnp.bfloat16)
    chunk = 256
    for t in range(0, count, chunk):
        rows = rows_ref[t : t + chunk, :]
        if kept_ref is not None:
            kept_ref[t : t + chunk, :] = rows
        square = jnp.square(rows.astype(jnp.float32))
        high = square.astype(jnp.bfloat16)
        low = (square - high.astype(jnp.float32)).astype(jnp.bfloat16)
        total = jnp.zeros((8, chunk), jnp.float32)
        for term in (high, low):
            total = total + lax.dot_general(
                ones, term, (((1,), (1,)), ((), ())), preferred_element_type=jnp.float32
            )
        bias_ref[:, t : t + chunk] = scale * total[0:1]


def norms(rows, scale, keep):
    in_vmem = pl.BlockSpec(memory_space=pltpu.VMEM)
    shapes = [jax.ShapeDtypeStruct((1, rows.shape[0]), jnp.float32)]
    if keep:
        shapes.append(jax.ShapeDtypeStruct(rows.shape, rows.dtype))
    return pl.pallas_call(
        functools.partial(norms_kernel, scale),
        out_shape=shapes,
        in_specs=[in_vmem],
        out_specs=[in_vmem] * len(shapes),
        compiler_params=pltpu.CompilerParams(vmem_limit_bytes=24 * 1024 * 1024),
        cost_estimate=pl.CostEstimate(
            flops=4 * 10**9, bytes_accessed=2 * rows.size * len(shapes), transcendentals=0
        ),
        name="norms",
    )(rows)


def score_kernel(n_sets, q_count, probe_count, n_active, scale, where_ref, *refs):
    q_refs = refs[:n_sets]
    sides = ((refs[n_sets], refs[n_sets + 2]), (refs[n_sets + 1], refs[n_sets + 3]))
    out_refs = refs[n_sets + 4 : 2 * n_sets + 4]
    held = refs[2 * n_sets + 4]
    half = sides[0][0].shape[0]
    block_total = 2 * half // BLK
    region = where_ref[0].astype(jnp.float32)
    columns = []
    for q_ref in q_refs:
        extra = q_ref.shape[0] - q_count
        tail = q_ref[...].astype(jnp.float32)[q_count:]
        tiles = -(-probe_count * (n_active + 1) // extra)
        meta = jnp.concatenate(
            [tail[:, i * q_count : (i + 1) * q_count] for i in range(tiles)], axis=0
        )
        wanted = jnp.zeros((n_active, q_count), jnp.float32)
        for p in range(probe_count):
            fine = meta[probe_count + p * n_active : probe_count + (p + 1) * n_active]
            wanted = wanted + jnp.where(meta[p : p + 1] == region, fine, 0.0)
        wanted = jnp.concatenate(
            [wanted, jnp.zeros((q_count - n_active, q_count), jnp.float32)], axis=0
        )
        columns.append(jnp.transpose(wanted).astype(jnp.int32) ^ (where_ref[1] * (block_total // 2)))
    rows = jnp.concatenate([r[0:q_count, :] for r in q_refs], axis=0)
    chunk = 512
    per = chunk // BLK
    step = 32
    places = [(side, t) for side in range(2) for t in range(0, half, chunk)]
    for i, (side, t) in enumerate(places):
        c_ref, b_ref = sides[side]
        inner = lax.dot_general(
            rows,
            c_ref[t : t + chunk, :],
            (((1,), (1,)), ((), ())),
            preferred_element_type=jnp.float32,
        )
        scored = inner + b_ref[:, t : t + chunk]
        for s in range(n_sets):
            for r in range(0, q_count, step):
                row = s * q_count + r
                options = [scored[row : row + step, b * BLK : (b + 1) * BLK] for b in range(per)]
                for j in range(n_active):
                    held[row : row + step, (i * n_active + j) * BLK : (i * n_active + j + 1) * BLK] = (
                        choose(options, columns[s][r : r + step, j : j + 1])
                    )
    for s in range(n_sets):
        for r in range(0, q_count, step):
            row = s * q_count + r
            for j in range(n_active):
                options = [
                    held[row : row + step, (i * n_active + j) * BLK : (i * n_active + j + 1) * BLK]
                    for i in range(len(places))
                ]
                best = choose(options, columns[s][r : r + step, j : j + 1], per)
                out_refs[s][r : r + step, j * BLK : (j + 1) * BLK] = (best * scale).astype(
                    jnp.bfloat16
                )


def score(where, blocks, own, other, own_bias, other_bias, q_count, probe_count, n_active, weight):
    n_sets = len(blocks)
    half, width = own.shape
    in_vmem = pl.BlockSpec(memory_space=pltpu.VMEM)
    out = jax.ShapeDtypeStruct((q_count, n_active * BLK), jnp.bfloat16)
    return pl.pallas_call(
        functools.partial(
            score_kernel, n_sets, q_count, probe_count, n_active, 1.0 / math.sqrt(width)
        ),
        out_shape=[out] * n_sets,
        in_specs=[pl.BlockSpec(memory_space=pltpu.SMEM)] + [in_vmem] * (n_sets + 4),
        out_specs=[in_vmem] * n_sets,
        scratch_shapes=[
            pltpu.VMEM((n_sets * q_count, 2 * half // 512 * n_active * BLK), jnp.float32)
        ],
        compiler_params=pltpu.CompilerParams(vmem_limit_bytes=24 * 1024 * 1024),
        cost_estimate=pl.CostEstimate(
            flops=weight * 2 * n_sets * q_count * 2 * half * width,
            bytes_accessed=2 * half * width * 2 + n_sets * q_count * (width + n_active * BLK) * 2,
            transcendentals=0,
        ),
        name="score",
    )(where, *blocks, own, other, own_bias, other_bias)


def answer_kernel(names, offset_ref, *refs):
    part_refs, base_ref, out_ref = refs[: len(names)], refs[len(names)], refs[-1]
    probe_count, q_count = offset_ref.shape
    length = part_refs[0].shape[1]
    offset = offset_ref[...].astype(jnp.float32)
    offset = jnp.concatenate(
        [offset, jnp.zeros((q_count - probe_count, q_count), jnp.float32)], axis=0
    )
    offset = jnp.transpose(offset).astype(jnp.int32)
    step = 16
    for r in range(0, q_count, step):
        parts = {n: p[r : r + step, :].astype(jnp.float32) for n, p in zip(names, part_refs)}
        for p in range(probe_count):
            column = offset[r : r + step, p : p + 1]
            place = slice(p * length, (p + 1) * length)
            if base_ref is out_ref:
                best = choose([parts.get(n, parts[names[0]]) for n in range(8)], column)
                out_ref[r : r + step, place] = best.astype(jnp.bfloat16)
            else:
                best = base_ref[r : r + step, place].astype(jnp.float32)
                for n in names:
                    best = jnp.where(column == n, parts[n], best)
                out_ref[r : r + step, p, :] = best.astype(jnp.bfloat16)


def answer(offset, parts, base=None):
    probe_count, q_count = offset.shape
    names = sorted(parts)
    length = parts[names[0]].shape[1]
    in_vmem = pl.BlockSpec(memory_space=pltpu.VMEM)
    inputs = [parts[n] for n in names] + ([] if base is None else [base])
    shape = (q_count, probe_count * length) if base is None else (q_count, probe_count, length)
    return pl.pallas_call(
        functools.partial(answer_kernel, names),
        out_shape=jax.ShapeDtypeStruct(shape, jnp.bfloat16),
        in_specs=[in_vmem] * (1 + len(inputs)),
        out_specs=in_vmem,
        compiler_params=pltpu.CompilerParams(vmem_limit_bytes=24 * 1024 * 1024),
        name="answer",
    )(offset, *inputs)


def by_blocks(queries, probes, fine_blocks, centroids):
    q_count, probe_count = probes.shape
    n_active = fine_blocks.shape[2]
    width = queries.shape[1]
    regions = lax.axis_size("region")

    def hop(value, mask):
        return lax.ppermute(value, "region", [(r, r ^ mask) for r in range(regions)])

    region = lax.axis_index("region")
    side = lax.axis_index("narrow")
    where = jnp.stack([region, side]).astype(jnp.int32)
    own = centroids[0]
    probes = probes.T
    fine = fine_blocks.reshape(q_count, -1).T
    held = {4: hop(queries, 4), 2: hop(queries, 2)}
    ids = list_ids(probes, fine)
    held[0] = pack(queries, ids, 8)
    held[1] = hop(held[0], 1)
    other = lax.ppermute(own, "narrow", [(0, 1), (1, 0)])
    factor = -0.5 / math.sqrt(width)
    (own_bias,) = norms(own, factor, False)
    other_bias, other = norms(other, factor, True)
    late_ids, own_bias, other_bias = lax.optimization_barrier((ids, own_bias, other_bias))
    ids_4, ids_2 = hop(late_ids, 4), hop(late_ids, 2)

    def scored(*keys, weight=1):
        blocks = [held[k] for k in keys]
        return score(
            where, blocks, own, other, own_bias, other_bias, q_count, probe_count, n_active, weight
        )

    barrier = lax.optimization_barrier
    results, back = {}, {}
    results[0], results[1] = scored(0, 1, weight=W01)
    held[4], held[2], ids_2, results[0] = barrier((held[4], held[2], ids_2, results[0]))
    held[4] = pack(held[4], ids_4, 8)
    held[2] = pack(held[2], ids_2, 8)
    held[6] = hop(held[4], 2)
    held[5] = hop(held[4], 1)
    results[4], results[2] = scored(4, 2, weight=W42)
    back[4] = hop(results[4], 4)
    results[1], results[4] = barrier((results[1], results[4]))
    back[1] = hop(results[1], 1)
    held[6], held[1], results[4] = barrier((held[6], held[1], results[4]))
    held[7] = hop(held[6], 1)
    held[3] = hop(held[1], 2)
    results[6], results[5] = scored(6, 5, weight=W56)
    back[6] = hop(results[6], 6)
    back[5] = hop(results[5], 5)
    results[2], results[5] = barrier((results[2], results[5]))
    back[2] = hop(results[2], 2)
    held[7], back[4], back[1] = barrier((held[7], back[4], back[1]))
    (results[7],) = scored(7, weight=W73)
    back[7] = hop(results[7], 7)
    held[3], results[7] = barrier((held[3], results[7]))
    (results[3],) = scored(3, weight=W73)
    back[3] = hop(results[3], 3)
    early = answer(probes ^ region, {0: results[0], **{k: back[k] for k in (1, 2, 4, 5, 6)}})
    probes, back[7] = barrier((probes, back[7]))
    return answer(probes ^ region, {3: back[3], 7: back[7]}, early)


def per_device(queries, probes, fine_blocks, centroids):
    q_count, probe_count = probes.shape
    regions = lax.axis_size("region")
    if regions == 8 and lax.axis_size("narrow") == 2 and 2 * probe_count >= regions:
        return by_blocks(queries, probes, fine_blocks, centroids)
    return by_slots(queries, probes, fine_blocks, centroids)


def solution(mesh):
    return jax.shard_map(
        per_device,
        mesh=mesh,
        in_specs=(
            P(("parts", "region", "narrow"), None),
            P(("parts", "region", "narrow"), None),
            P(("parts", "region", "narrow"), None, None),
            P("region", "narrow", None),
        ),
        out_specs=P(("parts", "region", "narrow"), None, None),
        check_vma=False,
    )
```
